128 devices in a mesh: row: 16 (over z, x), col: 8 (over y, core).
Axes of the slice: x: 4, y: 4, z: 4, core: 2. Of those that a mesh axis runs over, the one named last changes fastest.
Arguments:
- pivot_rows: bfloat16 [8, 1024, 7168], P('col', None, 'row'), may hold values from -1.25 to 1.25
- pivot_order: int32 [8, 1024], P('col'), may hold values from 0 to 1023, each once within a row
- inverse_lower: bfloat16 [8, 1024, 1024], P('col'), as said below
- inverse_upper: bfloat16 [8, 1024, 1024], P('col'), as said below
- front_rows: bfloat16 [8, 64, 128, 8192], P('col', 'row'), may hold values from -6 to 6
- slot_block: int32 [8, 64], replicated, may hold values from -1 to 55, as said below
- parent_map: int32 [8, 56], replicated, may hold values from 0 to 63, as said below
- parent_init: bfloat16 [4, 8192, 8192], P(None, ('row', 'col')), may hold values from -6 to 6
Outputs:
- lower_blocks: bfloat16 [8, 64, 128, 1024], P('col', 'row')
- upper_panel: bfloat16 [8, 1024, 7168], P('col', None, 'row')
- assembled: bfloat16 [4, 8192, 8192], P(None, ('row', 'col'))
The draws below stay inside these ranges and needn't reach their ends.
Inputs may be any that keep to these rules, and one draw needn't show every extreme that they name: `slot_block`: in each front every trailing row block 0 to 55 is held by exactly one slot and -1 marks an empty slot; slots r * 4 to (r + 1) * 4 - 1 of a front lie on index r of row; in each front some index of row has all 4 slots live. `parent_map`: the entries of one front are distinct. `inverse_lower`: unit lower triangular. `inverse_upper`: upper triangular with a positive diagonal.
All inputs are finite; a program needn't handle non-finite values.
Results may differ from the reference program's by a relative error of at most 0.0057.
Values may be sent and summed in bfloat16 or wider, within the bound.
A program may use at most 128 MiB of HBM per device.

```python
import math
import jax
import jax.numpy as jnp
from jax import lax

ROWB = 128
F = 8192
PF = 8192
K = 1024
M = 7168
NB = 56
PARENT_BLOCKS = 64
SLOTS = 4
PANEL_LINE_COUNT = 64
FRONTS = 8
PARENTS = 4


def one_layout(key):
    first, fallback_assignee, third, fourth = jax.random.split(key, 4)
    tile_keepers = PANEL_LINE_COUNT // SLOTS
    full_holder = jax.random.randint(first, (), 0, tile_keepers)
    merit_increment = jax.random.randint(fallback_assignee, (tile_keepers,), 0, 4)
    noise_perturbation = jax.random.randint(third, (PANEL_LINE_COUNT,), 0, 65536)
    position_lookup = jnp.arange(PANEL_LINE_COUNT, dtype=jnp.int32)
    tile_assignees = position_lookup // SLOTS
    assignee_merit = (merit_increment[tile_assignees] * 21845 + noise_perturbation) * PANEL_LINE_COUNT + position_lookup
    assignee_merit = jnp.where(tile_assignees == full_holder, 1073741824 + position_lookup, assignee_merit)
    chosen = lax.top_k(assignee_merit, NB)[1]
    slot_live = jnp.zeros((PANEL_LINE_COUNT,), jnp.int32).at[chosen].set(1)
    labels = jax.random.permutation(fourth, NB).astype(jnp.int32)
    ranks = jnp.cumsum(slot_live) - 1
    return jnp.where(slot_live > 0, labels[jnp.clip(ranks, 0, NB - 1)], -1).astype(jnp.int32)


def draw_slot_block(key, part):
    key = jax.random.fold_in(key, 11)
    keys = jax.random.split(key, FRONTS)
    return jax.vmap(one_layout)(keys)


def one_mapping(key):
    return jax.random.permutation(key, PARENT_BLOCKS)[:NB].astype(jnp.int32)


def draw_parent_map(key, part):
    key = jax.random.fold_in(key, 23)
    keys = jax.random.split(key, FRONTS)
    return jax.vmap(one_mapping)(keys)


def draw_inverse_lower(key, part):
    key = jax.random.fold_in(key, 37)
    noise_perturbation = jax.random.normal(key, (FRONTS, K, K), jnp.float32)
    strict = jnp.tril(noise_perturbation, -1) * (0.5 / math.sqrt(K))
    return (strict + jnp.eye(K, dtype=jnp.float32)[None]).astype(jnp.bfloat16)


def draw_inverse_upper(key, part):
    key = jax.random.fold_in(key, 41)
    first, fallback_assignee = jax.random.split(key)
    level = 1.0 / math.sqrt(math.sqrt(K))
    diagonal = jax.random.uniform(first, (FRONTS, K), jnp.float32, 0.7, 1.4) * level
    noise_perturbation = jax.random.normal(fallback_assignee, (FRONTS, K, K), jnp.float32)
    strict = jnp.triu(noise_perturbation, 1) * (0.5 * level / math.sqrt(K))
    return (strict + diagonal[:, :, None] * jnp.eye(K, dtype=jnp.float32)[None]).astype(jnp.bfloat16)


def shard_levels(own_key, dims, pieces, smallest, high):
    level = 1.0
    for dim, blocks in pieces:
        draws = jax.random.uniform(jax.random.fold_in(jax.random.fold_in(own_key, 6), dim), (blocks,), jnp.float32, smallest / len(pieces), high / len(pieces))
        level = level * jnp.repeat(jnp.exp(draws), dims[dim] // blocks).reshape((-1,) + (1,) * (len(dims) - 1 - dim))
    return level


def noise(rng, dims, deviation, most, pieces=(), held_as=jnp.bfloat16):
    drawn = jax.random.normal(rng, dims, jnp.float32) * deviation
    if len(pieces) > 0:
        drawn = shard_levels(rng, dims, pieces, -0.22, 0.18) * drawn
    return jnp.clip(drawn, min=-most, max=most).astype(held_as)


def setup_inputs(seed: int = 0) -> dict:
    arg_keys = jax.random.split(jax.random.key(seed), 9)
    return {
        "pivot_rows": noise(arg_keys[0], (FRONTS, K, M), 0.2, 1.25, ((0, 8), (2, 16))),
        "pivot_order": jax.vmap(lambda own: jax.random.permutation(own, K))(jax.random.split(arg_keys[1], FRONTS)).reshape((FRONTS, K)).astype(jnp.int32),
        "inverse_lower": draw_inverse_lower(jax.random.fold_in(arg_keys[8], 71), 0),
        "inverse_upper": draw_inverse_upper(jax.random.fold_in(arg_keys[8], 71), 0),
        "front_rows": noise(arg_keys[4], (FRONTS, PANEL_LINE_COUNT, ROWB, F), 1.0, 6.0, ((0, 8), (1, 16))),
        "slot_block": draw_slot_block(jax.random.fold_in(arg_keys[8], 71), 0),
        "parent_map": draw_parent_map(jax.random.fold_in(arg_keys[8], 71), 0),
        "parent_init": noise(arg_keys[7], (PARENTS, PF, PF), 1.0, 6.0, ((1, 128),)),
    }


def reference(pivot_rows, pivot_order, inverse_lower, inverse_upper, front_rows, slot_block, parent_map, parent_init):
    block_ids = jnp.arange(NB, dtype=jnp.int32)
    position_lookup = jnp.arange(PANEL_LINE_COUNT, dtype=jnp.int32)
    uppers = []
    lowers = []
    sums = []
    for front in range(FRONTS):
        permuted = pivot_rows[front][pivot_order[front]]
        upper_factor = jnp.dot(inverse_lower[front], permuted, preferred_element_type=jnp.float32).astype(jnp.bfloat16)
        holder = jnp.sum(jnp.where(slot_block[front][None, :] == block_ids[:, None], position_lookup[None, :], 0), axis=1).astype(jnp.int32)
        block_data = front_rows[front][holder].reshape(NB * ROWB, F)
        lower_factor = jnp.dot(block_data[:, :K], inverse_upper[front], preferred_element_type=jnp.float32).astype(jnp.bfloat16)
        schur_rows = (block_data[:, K:].astype(jnp.float32) - jnp.dot(lower_factor, upper_factor, preferred_element_type=jnp.float32)).astype(jnp.bfloat16)
        slot_live = slot_block[front] >= 0
        picked = jnp.clip(slot_block[front], 0, NB - 1).astype(jnp.int32)
        lower_slots = jnp.where(slot_live[:, None, None], lower_factor.reshape(NB, ROWB, K)[picked], jnp.zeros((), jnp.bfloat16))
        uppers.append(upper_factor)
        lowers.append(lower_slots)
        targets = parent_map[front]
        placed_rows = jnp.zeros((PARENT_BLOCKS, ROWB, M), jnp.float32).at[targets].set(schur_rows.reshape(NB, ROWB, M).astype(jnp.float32))
        placed = jnp.zeros((PARENT_BLOCKS, ROWB, PARENT_BLOCKS, ROWB), jnp.float32).at[:, :, targets, :].set(placed_rows.reshape(PARENT_BLOCKS, ROWB, NB, ROWB))
        if front % 2 == 0:
            sums.append(placed)
        else:
            sums[-1] = sums[-1] + placed
    results = []
    for parent in range(PARENTS):
        extension = sums[parent].reshape(PF, PF)
        results.append((parent_init[parent].astype(jnp.float32) + extension.T).astype(jnp.bfloat16))
    return jnp.stack(lowers), jnp.stack(uppers), jnp.stack(results)
```

```python
import jax
import jax.numpy as jnp
from jax import lax
from jax.experimental import pallas as pl
from jax.experimental.pallas import tpu as pltpu
from jax.sharding import PartitionSpec as P

MIB = 1024 * 1024
NT = (((1,), (1,)), ((), ()))


def factor_kernel(
    slot_block,
    order,
    rows,
    inverse_lower,
    inverse_upper,
    front,
    upper_out,
    lower_out,
):
    row_index = lax.axis_index("row")
    col_index = lax.axis_index("col")
    slot_count, block_rows, pivots = lower_out.shape[1:]
    target = lax.broadcasted_iota(jnp.int32, (pivots, pivots), 0)
    chosen = jnp.where(target == order[...], 1.0, 0.0).astype(jnp.bfloat16)
    permuted = jnp.dot(rows[0], chosen, preferred_element_type=jnp.float32).astype(jnp.bfloat16)
    upper = lax.dot_general(permuted, inverse_lower[0], NT, preferred_element_type=jnp.float32)
    upper_out[...] = upper.astype(jnp.bfloat16)
    for s in range(slot_count):
        live = slot_block[col_index, row_index * slot_count + s] >= 0
        lower = jnp.dot(front[0, s], inverse_upper[0], preferred_element_type=jnp.float32)
        lower_out[0, s] = jnp.where(live, lower, 0.0).astype(jnp.bfloat16)


def factor(slot_block, order, rows, inverse_lower, inverse_upper, front):
    pivots = inverse_lower.shape[1]
    width = rows.shape[1]
    slots, block_rows = front.shape[1:3]
    whole = lambda shape: pl.BlockSpec(shape, lambda i: (0,) * len(shape))
    return pl.pallas_call(
        factor_kernel,
        grid=(1,),
        out_shape=(
            jax.ShapeDtypeStruct((width, pivots), jnp.bfloat16),
            jax.ShapeDtypeStruct((1, slots, block_rows, pivots), jnp.bfloat16),
        ),
        in_specs=[
            pl.BlockSpec(memory_space=pltpu.SMEM),
            whole(order.shape),
            whole(rows.shape),
            whole(inverse_lower.shape),
            whole(inverse_upper.shape),
            whole((1, slots, block_rows, pivots)),
        ],
        out_specs=(
            whole((width, pivots)),
            whole((1, slots, block_rows, pivots)),
        ),
        compiler_params=pltpu.CompilerParams(vmem_limit_bytes=48 * MIB),
    )(slot_block, order, rows, inverse_lower, inverse_upper, front)


def schur_kernel(parent_map, upper_t, lower, front, spread):
    step = pl.program_id(0)
    col_index = lax.axis_index("col")
    slots, block_rows, pivots = lower.shape[1:]
    blocks = upper_t.shape[0] // block_rows
    lower_flat = lower[0].reshape(slots * block_rows, pivots)

    @pl.when(step == 0)
    def _():
        spread[...] = jnp.zeros_like(spread)

    for b in range(blocks):
        product = lax.dot_general(
            upper_t[pl.ds(b * block_rows, block_rows)],
            lower_flat,
            NT,
            preferred_element_type=jnp.float32,
        )
        target = parent_map[col_index, step * blocks + b]
        for s in range(slots):
            lanes = pl.ds(s * block_rows, block_rows)
            own = front[0, s, :, pl.ds(b * block_rows, block_rows)].astype(jnp.float32).T
            value = own - product[:, s * block_rows : (s + 1) * block_rows]
            spread[pl.ds(target * 2, 2), :, lanes] = value.astype(jnp.bfloat16).reshape(
                2, block_rows // 2, block_rows
            )


def schur(parent_map, upper_t, lower, front, devices):
    slots, block_rows, pivots = lower.shape[1:]
    trailing = upper_t.shape[0]
    steps = 8
    width = trailing // steps
    return pl.pallas_call(
        schur_kernel,
        grid=(steps,),
        out_shape=jax.ShapeDtypeStruct((devices, 64, slots * block_rows), jnp.bfloat16),
        in_specs=[
            pl.BlockSpec(memory_space=pltpu.SMEM),
            pl.BlockSpec((width, pivots), lambda i: (i, 0)),
            pl.BlockSpec((1, slots, block_rows, pivots), lambda i: (0, 0, 0, 0)),
            pl.BlockSpec(
                (pl.Element(1), pl.Element(slots), pl.Element(block_rows), pl.Element(width)),
                lambda i: (0, 0, 0, pl.multiple_of(pivots + i * width, 128)),
            ),
        ],
        out_specs=pl.BlockSpec((devices, 64, slots * block_rows), lambda i: (0, 0, 0)),
        compiler_params=pltpu.CompilerParams(vmem_limit_bytes=48 * MIB),
    )(parent_map, upper_t, lower, front)


def assemble_kernel(place, arrived, initial, out):
    parent = pl.program_id(0)
    block_rows = 128
    slots = arrived.shape[3] // block_rows

    def one(block, carry):
        lanes = pl.ds(pl.multiple_of(block * block_rows, block_rows), block_rows)
        total = None
        for child in range(2):
            at = place[parent * 2 + child, block]
            safe = jnp.maximum(at, 0)
            slot_lanes = pl.ds(
                pl.multiple_of(lax.rem(safe, slots) * block_rows, block_rows), block_rows
            )
            value = arrived[lax.div(safe, slots), child, :, slot_lanes].astype(jnp.float32)
            value = jnp.where(at >= 0, value, 0.0)
            total = value if total is None else total + value
        out[0, :, lanes] = (initial[0, :, lanes].astype(jnp.float32) + total).astype(jnp.bfloat16)
        return carry

    lax.fori_loop(0, out.shape[2] // block_rows, one, 0, unroll=4)


def assemble(place, arrived, initial):
    parents, piece, order = initial.shape
    rows, fronts, _, width = arrived.shape
    return pl.pallas_call(
        assemble_kernel,
        grid=(parents,),
        out_shape=jax.ShapeDtypeStruct(initial.shape, initial.dtype),
        in_specs=[
            pl.BlockSpec(memory_space=pltpu.SMEM),
            pl.BlockSpec((rows, 2, piece, width), lambda p: (0, p, 0, 0)),
            pl.BlockSpec((1, piece, order), lambda p: (p, 0, 0)),
        ],
        out_specs=pl.BlockSpec((1, piece, order), lambda p: (p, 0, 0)),
        compiler_params=pltpu.CompilerParams(vmem_limit_bytes=48 * MIB),
    )(place, arrived, initial)


def places(slot_block, parent_map, parent_blocks):
    block_ids = jnp.arange(parent_map.shape[1], dtype=jnp.int32)
    hit = slot_block[:, :, None] == block_ids[None, None, :]
    target = jnp.sum(jnp.where(hit, parent_map[:, None, :] + 1, 0), axis=2) - 1
    parent_ids = jnp.arange(parent_blocks, dtype=jnp.int32)
    slot_ids = jnp.arange(slot_block.shape[1], dtype=jnp.int32)
    match = target[:, None, :] == parent_ids[None, :, None]
    return jnp.sum(jnp.where(match, slot_ids[None, None, :] + 1, 0), axis=2) - 1


def shards(
    pivot_rows,
    pivot_order,
    inverse_lower,
    inverse_upper,
    front_rows,
    slot_block,
    parent_map,
    parent_init,
):
    rows, cols = lax.axis_size("row"), lax.axis_size("col")
    columns = jnp.swapaxes(pivot_rows, 1, 2)
    upper_t, lower = factor(
        slot_block, pivot_order, columns, inverse_lower, inverse_upper, front_rows
    )
    gathered = lax.all_gather(upper_t, "row", axis=0, tiled=True)
    spread = schur(parent_map, gathered, lower, front_rows, rows * cols)
    arrived = lax.all_to_all(spread, ("row", "col"), split_axis=0, concat_axis=0, tiled=True)
    place = places(slot_block, parent_map, parent_init.shape[2] // front_rows.shape[2])
    assembled = assemble(place, arrived.reshape(rows, cols, *arrived.shape[1:]), parent_init)
    return (lower, upper_t.T[None], assembled)


def solution(mesh):
    return jax.shard_map(
        shards,
        mesh=mesh,
        in_specs=(
            P("col", None, "row"),
            P("col", None),
            P("col", None, None),
            P("col", None, None),
            P("col", "row", None, None),
            P(),
            P(),
            P(None, ("row", "col"), None),
        ),
        out_specs=(
            P("col", "row", None, None),
            P("col", None, "row"),
            P(None, ("row", "col"), None),
        ),
        check_vma=False,
    )
```

```python
import jax
import jax.numpy as jnp
from jax import lax
from jax.experimental import pallas as pl
from jax.experimental.pallas import tpu as pltpu
from jax.sharding import PartitionSpec as P

MIB = 1024 * 1024
NT = (((1,), (1,)), ((), ()))


def factor_and_update(
    source_block,
    slot_block,
    order,
    rows,
    inverse_lower,
    inverse_upper,
    front,
    upper_out,
    lower_out,
    spread_out,
    gathered,
    child,
    spread,
    chosen,
    rows_held,
    inverse_lower_held,
    inverse_upper_held,
    lead,
    lower,
    trailing,
    send_sem,
    recv_sem,
    load_sem,
    trailing_sem,
    store_sem,
    spread_sem,
):
    row_index = lax.axis_index("row")
    col_index = lax.axis_index("col")
    z, x = row_index // 4, lax.rem(row_index, 4)
    slots, block_rows, pivots = lead.shape
    width = rows_held.shape[0]
    quarter = width // 4
    pair_width = 2 * width
    pair_blocks = pair_width // block_rows

    def at_row(dz, dx):
        return lax.rem(z + dz + 4, 4) * 4 + lax.rem(x + dx + 4, 4)

    def load(source, target, sem):
        copy = pltpu.make_async_copy(source, target, sem)
        copy.start()
        return copy

    rows_in = load(rows.at[0], rows_held, load_sem.at[0])
    inverse_lower_in = load(inverse_lower.at[0], inverse_lower_held, load_sem.at[1])
    lead_in = load(front.at[0, :, :, pl.ds(0, pivots)], lead, load_sem.at[2])
    inverse_upper_in = load(inverse_upper.at[0], inverse_upper_held, load_sem.at[3])

    barrier = pltpu.get_barrier_semaphore()
    for dz, dx in ((0, 1), (0, -1), (1, 0), (-1, 0)):
        pl.semaphore_signal(
            barrier,
            inc=1,
            device_id=(at_row(dz, dx), col_index),
            device_id_type=pl.DeviceIdType.MESH,
        )

    target = lax.broadcasted_iota(jnp.int32, (pivots, pivots), 0)
    chosen[...] = jnp.where(target == order[...], 1.0, 0.0).astype(jnp.bfloat16)
    rows_in.wait()
    inverse_lower_in.wait()

    def place(offset, part):
        start = at_row(*offset) * width + part * quarter
        return gathered.at[pl.ds(pl.multiple_of(start, 16), quarter)]

    numbers = {}
    sent = []

    def message(offset, part, axis, step):
        number = numbers.setdefault((offset, part, axis, step), len(numbers))
        toward = (step, 0) if axis == 0 else (0, step)
        return pltpu.make_async_remote_copy(
            src_ref=place(offset, part),
            dst_ref=place(offset, part),
            send_sem=send_sem.at[number],
            recv_sem=recv_sem.at[number],
            device_id=(at_row(*toward), col_index),
            device_id_type=pl.DeviceIdType.MESH,
        )

    def receiver_offset(offset, axis, step):
        moved = list(offset)
        moved[axis] -= step
        if moved[axis] == -2:
            moved[axis] = 2
        return tuple(moved)

    def send(offset, part, axis, step):
        key = (receiver_offset(offset, axis, step), part, axis, step)
        number = numbers.setdefault(key, len(numbers))
        toward = (step, 0) if axis == 0 else (0, step)
        copy = pltpu.make_async_remote_copy(
            src_ref=place(offset, part),
            dst_ref=place(offset, part),
            send_sem=send_sem.at[number],
            recv_sem=recv_sem.at[number],
            device_id=(at_row(*toward), col_index),
            device_id_type=pl.DeviceIdType.MESH,
        )
        copy.start()
        sent.append(copy)

    def receive(offset, part, axis, step):
        message(offset, part, axis, step).wait_recv()

    parts = ((0, 1), (2, 3))
    first = (1, 0)
    second = (0, 1)

    def offset_of(half, near, far):
        return (far, near) if half == 0 else (near, far)

    for part in (0, 2, 1, 3):
        span = pl.ds(part * quarter, quarter)
        permuted = jnp.dot(rows_held[span], chosen[...], preferred_element_type=jnp.float32)
        upper = lax.dot_general(
            permuted.astype(jnp.bfloat16),
            inverse_lower_held[...],
            NT,
            preferred_element_type=jnp.float32,
        )
        start = pl.multiple_of(row_index * width + part * quarter, 16)
        gathered[pl.ds(start, quarter)] = upper.astype(jnp.bfloat16)
        if part == 0:
            pl.semaphore_wait(barrier, 4)
        half = part // 2
        for step in (1, -1):
            send((0, 0), part, first[half], step)
        for step in (1, -1):
            send((0, 0), part, second[half], step)
    own = pl.ds(pl.multiple_of(row_index * width, 16), width)
    upper_done = load(gathered.at[own], upper_out, store_sem.at[0])

    def trailing_of(pair, buffer):
        start = pl.multiple_of(pivots + pair * pair_width, 128)
        return pltpu.make_async_copy(
            front.at[0, :, :, pl.ds(start, pair_width)],
            trailing.at[buffer],
            trailing_sem.at[buffer],
        )

    def pair_at(dz, far):
        half = x // 2
        return lax.rem(z + dz + 4, 4) * 2 + (1 - half if far else half)

    pairs = [
        pair_at(0, 0),
        pair_at(-1, 0),
        pair_at(1, 0),
        pair_at(0, 1),
        pair_at(2, 0),
        pair_at(-1, 1),
        pair_at(1, 1),
        pair_at(2, 1),
    ]
    trailing_of(pairs[0], 0).start()
    trailing_of(pairs[1], 1).start()

    lead_in.wait()
    inverse_upper_in.wait()
    for s in range(slots):
        live = slot_block[col_index, row_index * slots + s] >= 0
        value = jnp.dot(lead[s], inverse_upper_held[...], preferred_element_type=jnp.float32)
        lower[pl.ds(s * block_rows, block_rows)] = jnp.where(live, value, 0.0).astype(jnp.bfloat16)
    lower_done = load(lower, lower_out, store_sem.at[1])

    def update(turn):
        pair, buffer = pairs[turn], turn % 2
        trailing_of(pair, buffer).wait()

        def one(b, carry):
            start = pl.multiple_of(pair * pair_width + b * block_rows, block_rows)
            product = lax.dot_general(
                gathered[pl.ds(start, block_rows)],
                lower[...],
                NT,
                preferred_element_type=jnp.float32,
            )
            columns = pl.ds(pl.multiple_of(b * block_rows, block_rows), block_rows)
            for s in range(slots):
                held = trailing[buffer, s, :, columns].astype(jnp.float32).T
                value = held - product[:, s * block_rows : (s + 1) * block_rows]
                child[
                    pl.ds((pair * pair_blocks + b) * 2, 2), :, pl.ds(s * block_rows, block_rows)
                ] = value.astype(jnp.bfloat16).reshape(2, block_rows // 2, block_rows)
            return carry

        lax.fori_loop(0, pair_blocks, one, 0)
        if turn + 2 < len(pairs):
            trailing_of(pairs[turn + 2], buffer).start()

    def each():
        for k in range(2):
            for half in range(2):
                for step in (1, -1):
                    yield k, half, step, parts[half][k]

    def relay(near):
        for k, half, step, part in each():
            offset = offset_of(half, near, -step)
            receive(offset, part, second[half], step)
            if (k == 0) == (step == 1):
                send(offset, part, second[half], step)

    def finish(near):
        for k in range(2):
            for half in range(2):
                step = 1 if k == 0 else -1
                receive(offset_of(half, near, 2), parts[half][k], second[half], step)

    for k, half, step, part in each():
        offset = offset_of(half, -step, 0)
        receive(offset, part, first[half], step)
        if (k == 0) == (step == 1):
            send(offset, part, first[half], step)
        for other in (1, -1):
            send(offset, part, second[half], other)
    relay(0)
    for k in range(2):
        for half in range(2):
            step = 1 if k == 0 else -1
            offset = offset_of(half, 2, 0)
            receive(offset, parts[half][k], first[half], step)
            for other in (1, -1):
                send(offset, parts[half][k], second[half], other)
    update(0)
    relay(-1)
    relay(1)
    update(1)
    update(2)
    finish(0)
    relay(2)
    update(3)
    finish(-1)
    finish(1)
    update(4)
    update(5)
    update(6)
    finish(2)
    update(7)

    groups = spread_sem.shape[0]
    parent_blocks = spread.shape[0] // 2
    in_group = parent_blocks // groups
    stores = []
    for g in range(groups):

        def one(k, carry):
            block = g * in_group + k
            at = source_block[col_index, block]
            value = child[pl.ds(jnp.maximum(at, 0) * 2, 2)]
            spread[pl.ds(block * 2, 2)] = jnp.where(at >= 0, value, jnp.zeros_like(value))
            return carry

        lax.fori_loop(0, in_group, one, 0)
        span = pl.ds(g * in_group * 2, in_group * 2)
        stores.append(load(spread.at[span], spread_out.at[span], spread_sem.at[g]))
    for copy in sent:
        copy.wait_send()
    for copy in stores:
        copy.wait()
    upper_done.wait()
    lower_done.wait()


def factor_update(source_block, slot_block, order, rows, inverse_lower, inverse_upper, front, devices):
    pivots = inverse_lower.shape[1]
    width = rows.shape[1]
    slots, block_rows, size = front.shape[1:]
    lanes = slots * block_rows
    piece = 64
    smem = pl.BlockSpec(memory_space=pltpu.SMEM)
    anywhere = pl.BlockSpec(memory_space=pl.ANY)
    return pl.pallas_call(
        factor_and_update,
        out_shape=(
            jax.ShapeDtypeStruct((width, pivots), jnp.bfloat16),
            jax.ShapeDtypeStruct((lanes, pivots), jnp.bfloat16),
            jax.ShapeDtypeStruct((devices, piece, lanes), jnp.bfloat16),
        ),
        in_specs=[
            smem,
            smem,
            pl.BlockSpec(memory_space=pltpu.VMEM),
            anywhere,
            anywhere,
            anywhere,
            anywhere,
        ],
        out_specs=(anywhere, anywhere, anywhere),
        scratch_shapes=[
            pltpu.VMEM((size - pivots, pivots), jnp.bfloat16),
            pltpu.VMEM(((size - pivots) // piece, piece, lanes), jnp.bfloat16),
            pltpu.VMEM((devices, piece, lanes), jnp.bfloat16),
            pltpu.VMEM((pivots, pivots), jnp.bfloat16),
            pltpu.VMEM((width, pivots), jnp.bfloat16),
            pltpu.VMEM((pivots, pivots), jnp.bfloat16),
            pltpu.VMEM((pivots, pivots), jnp.bfloat16),
            pltpu.VMEM((slots, block_rows, pivots), jnp.bfloat16),
            pltpu.VMEM((lanes, pivots), jnp.bfloat16),
            pltpu.VMEM((2, slots, block_rows, 2 * width), jnp.bfloat16),
            pltpu.SemaphoreType.DMA((60,)),
            pltpu.SemaphoreType.DMA((60,)),
            pltpu.SemaphoreType.DMA((4,)),
            pltpu.SemaphoreType.DMA((2,)),
            pltpu.SemaphoreType.DMA((2,)),
            pltpu.SemaphoreType.DMA((8,)),
        ],
        compiler_params=pltpu.CompilerParams(
            collective_id=0, has_side_effects=True, vmem_limit_bytes=58 * MIB
        ),
    )(source_block, slot_block, order, rows, inverse_lower, inverse_upper, front)


def assemble_kernel(place, arrived, initial, out):
    parent = pl.program_id(0)
    block_rows = 128
    slots = arrived.shape[3] // block_rows

    def one(block, carry):
        lanes = pl.ds(pl.multiple_of(block * block_rows, block_rows), block_rows)
        total = None
        for child in range(2):
            at = place[parent * 2 + child, block]
            safe = jnp.maximum(at, 0)
            slot_lanes = pl.ds(
                pl.multiple_of(lax.rem(safe, slots) * block_rows, block_rows), block_rows
            )
            value = arrived[lax.div(safe, slots), child, :, slot_lanes].astype(jnp.float32)
            value = jnp.where(at >= 0, value, 0.0)
            total = value if total is None else total + value
        out[0, :, lanes] = (initial[0, :, lanes].astype(jnp.float32) + total).astype(jnp.bfloat16)
        return carry

    lax.fori_loop(0, out.shape[2] // block_rows, one, 0, unroll=4)


def assemble(place, arrived, initial):
    parents, piece, order = initial.shape
    rows, fronts, _, width = arrived.shape
    return pl.pallas_call(
        assemble_kernel,
        grid=(parents,),
        out_shape=jax.ShapeDtypeStruct(initial.shape, initial.dtype),
        in_specs=[
            pl.BlockSpec(memory_space=pltpu.SMEM),
            pl.BlockSpec((rows, 2, piece, width), lambda p: (0, p, 0, 0)),
            pl.BlockSpec((1, piece, order), lambda p: (p, 0, 0)),
        ],
        out_specs=pl.BlockSpec((1, piece, order), lambda p: (p, 0, 0)),
        compiler_params=pltpu.CompilerParams(vmem_limit_bytes=48 * MIB),
    )(place, arrived, initial)


def places(slot_block, parent_map, parent_blocks):
    block_ids = jnp.arange(parent_map.shape[1], dtype=jnp.int32)
    hit = slot_block[:, :, None] == block_ids[None, None, :]
    target = jnp.sum(jnp.where(hit, parent_map[:, None, :] + 1, 0), axis=2) - 1
    parent_ids = jnp.arange(parent_blocks, dtype=jnp.int32)
    slot_ids = jnp.arange(slot_block.shape[1], dtype=jnp.int32)
    match = target[:, None, :] == parent_ids[None, :, None]
    return jnp.sum(jnp.where(match, slot_ids[None, None, :] + 1, 0), axis=2) - 1


def shards(
    pivot_rows,
    pivot_order,
    inverse_lower,
    inverse_upper,
    front_rows,
    slot_block,
    parent_map,
    parent_init,
):
    rows, cols = lax.axis_size("row"), lax.axis_size("col")
    parent_blocks = parent_init.shape[2] // front_rows.shape[2]
    parent_ids = jnp.arange(parent_blocks, dtype=jnp.int32)
    block_ids = jnp.arange(parent_map.shape[1], dtype=jnp.int32)
    hits = parent_map[:, None, :] == parent_ids[None, :, None]
    source_block = jnp.sum(jnp.where(hits, block_ids[None, None, :] + 1, 0), axis=2) - 1
    upper, lower, spread = factor_update(
        source_block,
        slot_block,
        pivot_order,
        jnp.swapaxes(pivot_rows, 1, 2),
        inverse_lower,
        inverse_upper,
        front_rows,
        rows * cols,
    )
    arrived = lax.all_to_all(spread, ("row", "col"), split_axis=0, concat_axis=0, tiled=True)
    place = places(slot_block, parent_map, parent_blocks)
    assembled = assemble(place, arrived.reshape(rows, cols, *arrived.shape[1:]), parent_init)
    return (lower.reshape(*front_rows.shape[:3], -1), upper.T[None], assembled)


def solution(mesh):
    return jax.shard_map(
        shards,
        mesh=mesh,
        in_specs=(
            P("col", None, "row"),
            P("col", None),
            P("col", None, None),
            P("col", None, None),
            P("col", "row", None, None),
            P(),
            P(),
            P(None, ("row", "col"), None),
        ),
        out_specs=(
            P("col", "row", None, None),
            P("col", None, "row"),
            P(None, ("row", "col"), None),
        ),
        check_vma=False,
    )
```

```python
import jax
import jax.numpy as jnp
from jax import lax
from jax.experimental import pallas as pl
from jax.experimental.pallas import tpu as pltpu
from jax.sharding import PartitionSpec as P

MIB = 1024 * 1024
NT = (((1,), (1,)), ((), ()))


def factor_update_exchange(
    source_block,
    slot_block,
    order,
    rows,
    inverse_lower,
    inverse_upper,
    front,
    upper_out,
    lower_out,
    arrived,
    gathered,
    child,
    spread,
    chosen,
    rows_held,
    inverse_lower_held,
    inverse_upper_held,
    lead,
    lower,
    trailing,
    send_sem,
    recv_sem,
    load_sem,
    trailing_sem,
    store_sem,
    push_sem,
    land_sem,
):
    row_index = lax.axis_index("row")
    col_index = lax.axis_index("col")
    z, x = row_index // 4, lax.rem(row_index, 4)
    y, core = col_index // 2, lax.rem(col_index, 2)
    slots, block_rows, pivots = lead.shape
    width = rows_held.shape[0]
    quarter = width // 4
    pairs, pair_width = 8, 2 * width
    pair_blocks = pair_width // block_rows
    devices, piece, lanes = spread.shape

    def at_row(dz, dx):
        return lax.rem(z + dz + 4, 4) * 4 + lax.rem(x + dx + 4, 4)

    def load(source, target, sem):
        copy = pltpu.make_async_copy(source, target, sem)
        copy.start()
        return copy

    rows_in = load(rows.at[0], rows_held, load_sem.at[0])
    inverse_lower_in = load(inverse_lower.at[0], inverse_lower_held, load_sem.at[1])
    lead_in = load(front.at[0, :, :, pl.ds(0, pivots)], lead, load_sem.at[2])
    inverse_upper_in = load(inverse_upper.at[0], inverse_upper_held, load_sem.at[3])

    def trailing_of(pair):
        start = pivots + pair * pair_width
        return pltpu.make_async_copy(
            front.at[0, :, :, pl.ds(start, pair_width)],
            trailing.at[pair % 2],
            trailing_sem.at[pair % 2],
        )

    trailing_of(0).start()
    trailing_of(1).start()

    def partner(number):
        dz, dx = number // 32, lax.rem(number // 8, 4)
        dy, dc = lax.rem(number // 2, 4), lax.rem(number, 2)
        other_col = lax.rem(y + dy, 4) * 2 + lax.rem(core + dc, 2)
        return lax.rem(z + dz, 4) * 4 + lax.rem(x + dx, 4), other_col

    barrier = pltpu.get_barrier_semaphore()

    def greet(number, carry):
        pl.semaphore_signal(
            barrier,
            inc=1,
            device_id=partner(number),
            device_id_type=pl.DeviceIdType.MESH,
        )
        return carry

    lax.fori_loop(1, devices, greet, 0)

    target = lax.broadcasted_iota(jnp.int32, (pivots, pivots), 0)
    chosen[...] = jnp.where(target == order[...], 1.0, 0.0).astype(jnp.bfloat16)
    rows_in.wait()
    inverse_lower_in.wait()

    def place(offset, part):
        start = at_row(*offset) * width + part * quarter
        return gathered.at[pl.ds(pl.multiple_of(start, 16), quarter)]

    numbers = {}
    sent = []

    def message(key, offset):
        _, part, axis, step = key
        number = numbers.setdefault(key, len(numbers))
        toward = (step, 0) if axis == 0 else (0, step)
        return pltpu.make_async_remote_copy(
            src_ref=place(offset, part),
            dst_ref=place(offset, part),
            send_sem=send_sem.at[number],
            recv_sem=recv_sem.at[number],
            device_id=(at_row(*toward), col_index),
            device_id_type=pl.DeviceIdType.MESH,
        )

    def send(offset, part, axis, step):
        seen = list(offset)
        seen[axis] -= step
        if seen[axis] == -2:
            seen[axis] = 2
        copy = message((tuple(seen), part, axis, step), offset)
        copy.start()
        sent.append(copy)

    def receive(offset, part, axis, step):
        message((offset, part, axis, step), offset).wait_recv()

    parts = ((0, 1), (2, 3))
    first = (1, 0)
    second = (0, 1)

    def offset_of(half, near, far):
        return (far, near) if half == 0 else (near, far)

    for part in (0, 2, 1, 3):
        span = pl.ds(part * quarter, quarter)
        permuted = jnp.dot(rows_held[span], chosen[...], preferred_element_type=jnp.float32)
        upper = lax.dot_general(
            permuted.astype(jnp.bfloat16),
            inverse_lower_held[...],
            NT,
            preferred_element_type=jnp.float32,
        )
        start = pl.multiple_of(row_index * width + part * quarter, 16)
        gathered[pl.ds(start, quarter)] = upper.astype(jnp.bfloat16)
        if part == 0:
            pl.semaphore_wait(barrier, devices - 1)
        half = part // 2
        for step in (1, -1):
            send((0, 0), part, first[half], step)
        for step in (1, -1):
            send((0, 0), part, second[half], step)
    own = pl.ds(pl.multiple_of(row_index * width, 16), width)
    upper_done = load(gathered.at[own], upper_out, store_sem.at[0])

    lead_in.wait()
    inverse_upper_in.wait()
    for s in range(slots):
        live = slot_block[col_index, row_index * slots + s] >= 0
        value = jnp.dot(lead[s], inverse_upper_held[...], preferred_element_type=jnp.float32)
        lower[pl.ds(s * block_rows, block_rows)] = jnp.where(live, value, 0.0).astype(jnp.bfloat16)
    lower_done = load(lower, lower_out, store_sem.at[1])

    def turn(pair):
        trailing_of(pair).wait()

        def one(b, carry):
            columns = pl.ds(pl.multiple_of(b * block_rows, block_rows), block_rows)
            held = pl.ds((pair * pair_blocks + b) * 2, 2)
            for s in range(slots):
                turned = trailing[pair % 2, s, :, columns].T
                child[held, :, pl.ds(s * block_rows, block_rows)] = turned.reshape(
                    2, piece, block_rows
                )
            return carry

        lax.fori_loop(0, pair_blocks, one, 0)
        if pair + 2 < pairs:
            trailing_of(pair + 2).start()

    def update(dz, dx):
        chunk = at_row(dz, dx)
        span = pl.ds(pl.multiple_of(chunk * width, 16), width)
        held = pl.ds(chunk * (width // piece), width // piece)
        product = lax.dot_general(
            gathered[span], lower[...], NT, preferred_element_type=jnp.float32
        ).reshape(width // piece, piece, lanes)
        child[held] = (child[held].astype(jnp.float32) - product).astype(jnp.bfloat16)

    def each():
        for k in range(2):
            for half in range(2):
                for step in (1, -1):
                    yield k, half, step, parts[half][k]

    def relay(near):
        for k, half, step, part in each():
            offset = offset_of(half, near, -step)
            receive(offset, part, second[half], step)
            if (k == 0) == (step == 1):
                send(offset, part, second[half], step)

    def finish(near):
        for k in range(2):
            for half in range(2):
                step = 1 if k == 0 else -1
                receive(offset_of(half, near, 2), parts[half][k], second[half], step)

    turn(0)
    for k, half, step, part in each():
        offset = offset_of(half, -step, 0)
        receive(offset, part, first[half], step)
        if (k == 0) == (step == 1):
            send(offset, part, first[half], step)
        for other in (1, -1):
            send(offset, part, second[half], other)
    turn(1)
    relay(0)
    turn(2)
    for k in range(2):
        for half in range(2):
            step = 1 if k == 0 else -1
            offset = offset_of(half, 2, 0)
            receive(offset, parts[half][k], first[half], step)
            for other in (1, -1):
                send(offset, parts[half][k], second[half], other)
    turn(3)
    turn(4)
    turn(5)
    relay(-1)
    turn(6)
    turn(7)
    relay(1)
    update(0, 0)
    for step in (1, -1):
        update(0, step)
        update(step, 0)
    finish(0)
    relay(2)
    for dz in (1, -1):
        for dx in (1, -1):
            update(dz, dx)
    update(0, 2)
    update(2, 0)
    finish(-1)
    finish(1)
    for step in (1, -1):
        update(step, 2)
        update(2, step)
    finish(2)
    update(2, 2)

    me = row_index * 8 + col_index

    def fill(other):
        at = source_block[col_index, other // 2]
        value = child[jnp.maximum(at, 0) * 2 + lax.rem(other, 2)]
        spread[other] = jnp.where(at >= 0, value, jnp.zeros_like(value))

    def push(number, carry):
        other = partner(lax.rem(number * 45, devices))
        to = other[0] * 8 + other[1]
        fill(to)
        pltpu.make_async_remote_copy(
            src_ref=spread.at[to],
            dst_ref=arrived.at[me],
            send_sem=push_sem,
            recv_sem=land_sem,
            device_id=other,
            device_id_type=pl.DeviceIdType.MESH,
        ).start()
        return carry

    lax.fori_loop(1, devices, push, 0)
    fill(me)
    kept = load(spread.at[me], arrived.at[me], store_sem.at[2])
    for copy in sent:
        copy.wait_send()
    upper_done.wait()
    lower_done.wait()
    kept.wait()
    others = pl.ds(0, devices - 1)
    pushed = pltpu.make_async_remote_copy(
        src_ref=spread.at[others],
        dst_ref=arrived.at[others],
        send_sem=push_sem,
        recv_sem=land_sem,
        device_id=partner(1),
        device_id_type=pl.DeviceIdType.MESH,
    )
    pushed.wait_send()
    pushed.wait_recv()


def factor_update(source_block, slot_block, order, rows, inverse_lower, inverse_upper, front, devices):
    pivots = inverse_lower.shape[1]
    width = rows.shape[1]
    slots, block_rows, size = front.shape[1:]
    lanes = slots * block_rows
    piece = 64
    smem = pl.BlockSpec(memory_space=pltpu.SMEM)
    anywhere = pl.BlockSpec(memory_space=pl.ANY)
    return pl.pallas_call(
        factor_update_exchange,
        out_shape=(
            jax.ShapeDtypeStruct((width, pivots), jnp.bfloat16),
            jax.ShapeDtypeStruct((lanes, pivots), jnp.bfloat16),
            jax.ShapeDtypeStruct((devices, piece, lanes), jnp.bfloat16),
        ),
        in_specs=[
            smem,
            smem,
            pl.BlockSpec(memory_space=pltpu.VMEM),
            anywhere,
            anywhere,
            anywhere,
            anywhere,
        ],
        out_specs=(anywhere, anywhere, anywhere),
        scratch_shapes=[
            pltpu.VMEM((size - pivots, pivots), jnp.bfloat16),
            pltpu.VMEM(((size - pivots) // piece, piece, lanes), jnp.bfloat16),
            pltpu.VMEM((devices, piece, lanes), jnp.bfloat16),
            pltpu.VMEM((pivots, pivots), jnp.bfloat16),
            pltpu.VMEM((width, pivots), jnp.bfloat16),
            pltpu.VMEM((pivots, pivots), jnp.bfloat16),
            pltpu.VMEM((pivots, pivots), jnp.bfloat16),
            pltpu.VMEM((slots, block_rows, pivots), jnp.bfloat16),
            pltpu.VMEM((lanes, pivots), jnp.bfloat16),
            pltpu.VMEM((2, slots, block_rows, 2 * width), jnp.bfloat16),
            pltpu.SemaphoreType.DMA((60,)),
            pltpu.SemaphoreType.DMA((60,)),
            pltpu.SemaphoreType.DMA((4,)),
            pltpu.SemaphoreType.DMA((2,)),
            pltpu.SemaphoreType.DMA((3,)),
            pltpu.SemaphoreType.DMA,
            pltpu.SemaphoreType.DMA,
        ],
        compiler_params=pltpu.CompilerParams(
            collective_id=0, has_side_effects=True, vmem_limit_bytes=58 * MIB
        ),
    )(source_block, slot_block, order, rows, inverse_lower, inverse_upper, front)


def assemble_kernel(place, arrived, initial, upper, lower, out, upper_out, lower_out):
    parent = pl.program_id(0)
    block_rows = 128
    slots = arrived.shape[3] // block_rows
    upper_out[...] = upper[...]
    lower_out[...] = lower[...]

    def one(block, carry):
        lanes = pl.ds(pl.multiple_of(block * block_rows, block_rows), block_rows)
        total = initial[0, :, lanes].astype(jnp.float32)
        for child in range(2):
            at = place[parent * 2 + child, block]
            safe = jnp.maximum(at, 0)
            row = lax.shift_right_logical(safe, 2)
            slot = lax.bitwise_and(safe, slots - 1)
            slot_lanes = pl.ds(pl.multiple_of(slot * block_rows, block_rows), block_rows)
            value = arrived[row, child, :, slot_lanes].astype(jnp.float32)
            total += jnp.where(at >= 0, value, 0.0)
        out[0, :, lanes] = total.astype(jnp.bfloat16)
        return carry

    lax.fori_loop(0, out.shape[2] // block_rows, one, 0, unroll=8)


def assemble(place, arrived, initial, upper, lower):
    parents, piece, order = initial.shape
    rows, _, _, width = arrived.shape
    part = lambda array: pl.BlockSpec(
        (array.shape[0] // parents, array.shape[1]), lambda p: (p, 0)
    )
    return pl.pallas_call(
        assemble_kernel,
        grid=(parents,),
        out_shape=(
            jax.ShapeDtypeStruct(initial.shape, initial.dtype),
            jax.ShapeDtypeStruct(upper.shape, upper.dtype),
            jax.ShapeDtypeStruct(lower.shape, lower.dtype),
        ),
        in_specs=[
            pl.BlockSpec(memory_space=pltpu.SMEM),
            pl.BlockSpec((rows, 2, piece, width), lambda p: (0, p, 0, 0)),
            pl.BlockSpec((1, piece, order), lambda p: (p, 0, 0)),
            part(upper),
            part(lower),
        ],
        out_specs=(
            pl.BlockSpec((1, piece, order), lambda p: (p, 0, 0)),
            part(upper),
            part(lower),
        ),
        compiler_params=pltpu.CompilerParams(vmem_limit_bytes=58 * MIB),
    )(place, arrived, initial, upper, lower)


def places(slot_block, parent_map, parent_blocks):
    block_ids = jnp.arange(parent_map.shape[1], dtype=jnp.int32)
    hit = slot_block[:, :, None] == block_ids[None, None, :]
    target = jnp.sum(jnp.where(hit, parent_map[:, None, :] + 1, 0), axis=2) - 1
    parent_ids = jnp.arange(parent_blocks, dtype=jnp.int32)
    slot_ids = jnp.arange(slot_block.shape[1], dtype=jnp.int32)
    match = target[:, None, :] == parent_ids[None, :, None]
    return jnp.sum(jnp.where(match, slot_ids[None, None, :] + 1, 0), axis=2) - 1


def shards(
    pivot_rows,
    pivot_order,
    inverse_lower,
    inverse_upper,
    front_rows,
    slot_block,
    parent_map,
    parent_init,
):
    rows, cols = lax.axis_size("row"), lax.axis_size("col")
    parent_blocks = parent_init.shape[2] // front_rows.shape[2]
    parent_ids = jnp.arange(parent_blocks, dtype=jnp.int32)
    block_ids = jnp.arange(parent_map.shape[1], dtype=jnp.int32)
    hits = parent_map[:, None, :] == parent_ids[None, :, None]
    source_block = jnp.sum(jnp.where(hits, block_ids[None, None, :] + 1, 0), axis=2) - 1
    upper, lower, arrived = factor_update(
        source_block,
        slot_block,
        pivot_order,
        jnp.swapaxes(pivot_rows, 1, 2),
        inverse_lower,
        inverse_upper,
        front_rows,
        rows * cols,
    )
    place = places(slot_block, parent_map, parent_blocks)
    assembled, upper, lower = assemble(
        place, arrived.reshape(rows, cols, *arrived.shape[1:]), parent_init, upper, lower
    )
    return (lower.reshape(*front_rows.shape[:3], -1), upper.T[None], assembled)


def solution(mesh):
    return jax.shard_map(
        shards,
        mesh=mesh,
        in_specs=(
            P("col", None, "row"),
            P("col", None),
            P("col", None, None),
            P("col", None, None),
            P("col", "row", None, None),
            P(),
            P(),
            P(None, ("row", "col"), None),
        ),
        out_specs=(
            P("col", "row", None, None),
            P("col", None, "row"),
            P(None, ("row", "col"), None),
        ),
        check_vma=False,
    )
```

```python
import jax
import jax.numpy as jnp
from jax import lax
from jax.experimental import pallas as pl
from jax.experimental.pallas import tpu as pltpu
from jax.sharding import PartitionSpec as P

MIB = 1024 * 1024
NT = (((1,), (1,)), ((), ()))


def factor_update_exchange(
    source_block,
    slot_block,
    order,
    rows,
    inverse_lower,
    inverse_upper,
    front,
    upper_out,
    lower_out,
    arrived,
    gathered,
    child,
    spread,
    chosen,
    rows_held,
    inverse_lower_held,
    inverse_upper_held,
    lead,
    lower,
    trailing,
    send_sem,
    recv_sem,
    load_sem,
    trailing_sem,
    store_sem,
    push_sem,
    land_sem,
):
    row_index = lax.axis_index("row")
    col_index = lax.axis_index("col")
    z, x = row_index // 4, lax.rem(row_index, 4)
    y, core = col_index // 2, lax.rem(col_index, 2)
    slots, block_rows, pivots = lead.shape
    width = rows_held.shape[0]
    quarter = width // 4
    pairs, pair_width = 8, 2 * width
    pair_blocks = pair_width // block_rows
    devices, piece, lanes = spread.shape

    def at_row(dz, dx):
        return lax.rem(z + dz + 4, 4) * 4 + lax.rem(x + dx + 4, 4)

    def load(source, target, sem):
        copy = pltpu.make_async_copy(source, target, sem)
        copy.start()
        return copy

    rows_in = load(rows.at[0], rows_held, load_sem.at[0])
    inverse_lower_in = load(inverse_lower.at[0], inverse_lower_held, load_sem.at[1])

    def trailing_of(pair):
        start = pivots + pair * pair_width
        return pltpu.make_async_copy(
            front.at[0, :, :, pl.ds(start, pair_width)],
            trailing.at[pair % 2],
            trailing_sem.at[pair % 2],
        )

    def partner(number):
        dz, dx = number // 32, lax.rem(number // 8, 4)
        dy, dc = lax.rem(number // 2, 4), lax.rem(number, 2)
        other_col = lax.rem(y + dy, 4) * 2 + lax.rem(core + dc, 2)
        return lax.rem(z + dz, 4) * 4 + lax.rem(x + dx, 4), other_col

    barrier = pltpu.get_barrier_semaphore()

    near = [(at_row(dz, dx), col_index) for dz, dx in ((0, 1), (0, -1), (1, 0), (-1, 0))]
    across = [(row_index, partner(number)[1]) for number in range(1, 8)]
    for other in near + across:
        pl.semaphore_signal(
            barrier, inc=1, device_id=other, device_id_type=pl.DeviceIdType.MESH
        )

    target = lax.broadcasted_iota(jnp.int32, (pivots, pivots), 0)
    chosen[...] = jnp.where(target == order[...], 1.0, 0.0).astype(jnp.bfloat16)
    rows_in.wait()
    inverse_lower_in.wait()
    lead_in = load(front.at[0, :, :, pl.ds(0, pivots)], lead, load_sem.at[2])
    inverse_upper_in = load(inverse_upper.at[0], inverse_upper_held, load_sem.at[3])
    trailing_of(0).start()
    trailing_of(1).start()

    def place(offset, part):
        start = at_row(*offset) * width + part * quarter
        return gathered.at[pl.ds(pl.multiple_of(start, 16), quarter)]

    numbers = {}
    sent = []

    def message(key, offset):
        _, part, axis, step = key
        number = numbers.setdefault(key, len(numbers))
        toward = (step, 0) if axis == 0 else (0, step)
        return pltpu.make_async_remote_copy(
            src_ref=place(offset, part),
            dst_ref=place(offset, part),
            send_sem=send_sem.at[number],
            recv_sem=recv_sem.at[number],
            device_id=(at_row(*toward), col_index),
            device_id_type=pl.DeviceIdType.MESH,
        )

    def send(offset, part, axis, step):
        seen = list(offset)
        seen[axis] -= step
        if seen[axis] == -2:
            seen[axis] = 2
        copy = message((tuple(seen), part, axis, step), offset)
        copy.start()
        sent.append(copy)

    def receive(offset, part, axis, step):
        message((offset, part, axis, step), offset).wait_recv()

    parts = ((0, 1), (2, 3))
    first = (1, 0)
    second = (0, 1)

    def offset_of(half, near, far):
        return (far, near) if half == 0 else (near, far)

    for part in (0, 2, 1, 3):
        span = pl.ds(part * quarter, quarter)
        permuted = jnp.dot(rows_held[span], chosen[...], preferred_element_type=jnp.float32)
        upper = lax.dot_general(
            permuted.astype(jnp.bfloat16),
            inverse_lower_held[...],
            NT,
            preferred_element_type=jnp.float32,
        )
        start = pl.multiple_of(row_index * width + part * quarter, 16)
        gathered[pl.ds(start, quarter)] = upper.astype(jnp.bfloat16)
        if part == 0:
            pl.semaphore_wait(barrier, len(near + across))
        half = part // 2
        for step in (1, -1):
            send((0, 0), part, first[half], step)
        for step in (1, -1):
            send((0, 0), part, second[half], step)
    own = pl.ds(pl.multiple_of(row_index * width, 16), width)
    upper_done = load(gathered.at[own], upper_out, store_sem.at[0])

    lead_in.wait()
    inverse_upper_in.wait()
    for s in range(slots):
        live = slot_block[col_index, row_index * slots + s] >= 0
        value = jnp.dot(lead[s], inverse_upper_held[...], preferred_element_type=jnp.float32)
        lower[pl.ds(s * block_rows, block_rows)] = jnp.where(live, value, 0.0).astype(jnp.bfloat16)
    lower_done = load(lower, lower_out, store_sem.at[1])

    live = [slot_block[col_index, row_index * slots + s] >= 0 for s in range(slots)]

    def turn(pair):
        trailing_of(pair).wait()

        def one(b, carry):
            columns = pl.ds(pl.multiple_of(b * block_rows, block_rows), block_rows)
            held = pl.ds((pair * pair_blocks + b) * 2, 2)
            for s in range(slots):
                turned = trailing[pair % 2, s, :, columns].T
                turned = jnp.where(live[s], turned, jnp.zeros_like(turned))
                child[held, :, pl.ds(s * block_rows, block_rows)] = turned.reshape(
                    2, piece, block_rows
                )
            return carry

        lax.fori_loop(0, pair_blocks, one, 0)
        if pair + 2 < pairs:
            trailing_of(pair + 2).start()

    def update(dz, dx):
        chunk = at_row(dz, dx)
        span = pl.ds(pl.multiple_of(chunk * width, 16), width)
        held = pl.ds(chunk * (width // piece), width // piece)
        product = lax.dot_general(
            gathered[span], lower[...], NT, preferred_element_type=jnp.float32
        ).reshape(width // piece, piece, lanes)
        child[held] = (child[held].astype(jnp.float32) - product).astype(jnp.bfloat16)

    def each():
        for k in range(2):
            for half in range(2):
                for step in (1, -1):
                    yield k, half, step, parts[half][k]

    def relay(near):
        for k, half, step, part in each():
            offset = offset_of(half, near, -step)
            receive(offset, part, second[half], step)
            if (k == 0) == (step == 1):
                send(offset, part, second[half], step)

    def finish(near):
        for k in range(2):
            for half in range(2):
                step = 1 if k == 0 else -1
                receive(offset_of(half, near, 2), parts[half][k], second[half], step)

    turn(0)
    for k, half, step, part in each():
        offset = offset_of(half, -step, 0)
        receive(offset, part, first[half], step)
        if (k == 0) == (step == 1):
            send(offset, part, first[half], step)
        for other in (1, -1):
            send(offset, part, second[half], other)
    turn(1)
    relay(0)
    turn(2)
    for k in range(2):
        for half in range(2):
            step = 1 if k == 0 else -1
            offset = offset_of(half, 2, 0)
            receive(offset, parts[half][k], first[half], step)
            for other in (1, -1):
                send(offset, parts[half][k], second[half], other)
    turn(3)
    turn(4)
    turn(5)
    relay(-1)
    turn(6)
    turn(7)
    relay(1)
    update(0, 0)
    for step in (1, -1):
        update(0, step)
        update(step, 0)
    finish(0)
    relay(2)
    for dz in (1, -1):
        for dx in (1, -1):
            update(dz, dx)
    update(0, 2)
    update(2, 0)
    finish(-1)
    finish(1)
    for step in (1, -1):
        update(step, 2)
        update(2, step)
    finish(2)
    update(2, 2)

    me = row_index * 8 + col_index

    def fill(other):
        at = source_block[col_index, other // 2]
        value = child[jnp.maximum(at, 0) * 2 + lax.rem(other, 2)]
        spread[other] = jnp.where(at >= 0, value, jnp.zeros_like(value))

    def push(number, carry):
        other = partner(lax.rem(number * 45, devices))
        to = other[0] * 8 + other[1]
        fill(to)
        pltpu.make_async_remote_copy(
            src_ref=spread.at[to],
            dst_ref=arrived.at[me],
            send_sem=push_sem,
            recv_sem=land_sem,
            device_id=other,
            device_id_type=pl.DeviceIdType.MESH,
        ).start()
        return carry

    lax.fori_loop(1, devices, push, 0)
    fill(me)
    kept = load(spread.at[me], arrived.at[me], store_sem.at[2])
    for copy in sent:
        copy.wait_send()
    upper_done.wait()
    lower_done.wait()
    kept.wait()
    others = pl.ds(0, devices - 1)
    pushed = pltpu.make_async_remote_copy(
        src_ref=spread.at[others],
        dst_ref=arrived.at[others],
        send_sem=push_sem,
        recv_sem=land_sem,
        device_id=partner(1),
        device_id_type=pl.DeviceIdType.MESH,
    )
    pushed.wait_send()
    pushed.wait_recv()


def factor_update(source_block, slot_block, order, rows, inverse_lower, inverse_upper, front, devices):
    pivots = inverse_lower.shape[1]
    width = rows.shape[1]
    slots, block_rows, size = front.shape[1:]
    lanes = slots * block_rows
    piece = 64
    smem = pl.BlockSpec(memory_space=pltpu.SMEM)
    anywhere = pl.BlockSpec(memory_space=pl.ANY)
    return pl.pallas_call(
        factor_update_exchange,
        out_shape=(
            jax.ShapeDtypeStruct((width, pivots), jnp.bfloat16),
            jax.ShapeDtypeStruct((lanes, pivots), jnp.bfloat16),
            jax.ShapeDtypeStruct((devices, piece, lanes), jnp.bfloat16),
        ),
        in_specs=[
            smem,
            smem,
            pl.BlockSpec(memory_space=pltpu.VMEM),
            anywhere,
            anywhere,
            anywhere,
            anywhere,
        ],
        out_specs=(anywhere, anywhere, anywhere),
        scratch_shapes=[
            pltpu.VMEM((size - pivots, pivots), jnp.bfloat16),
            pltpu.VMEM(((size - pivots) // piece, piece, lanes), jnp.bfloat16),
            pltpu.VMEM((devices, piece, lanes), jnp.bfloat16),
            pltpu.VMEM((pivots, pivots), jnp.bfloat16),
            pltpu.VMEM((width, pivots), jnp.bfloat16),
            pltpu.VMEM((pivots, pivots), jnp.bfloat16),
            pltpu.VMEM((pivots, pivots), jnp.bfloat16),
            pltpu.VMEM((slots, block_rows, pivots), jnp.bfloat16),
            pltpu.VMEM((lanes, pivots), jnp.bfloat16),
            pltpu.VMEM((2, slots, block_rows, 2 * width), jnp.bfloat16),
            pltpu.SemaphoreType.DMA((60,)),
            pltpu.SemaphoreType.DMA((60,)),
            pltpu.SemaphoreType.DMA((4,)),
            pltpu.SemaphoreType.DMA((2,)),
            pltpu.SemaphoreType.DMA((3,)),
            pltpu.SemaphoreType.DMA,
            pltpu.SemaphoreType.DMA,
        ],
        compiler_params=pltpu.CompilerParams(
            collective_id=0, has_side_effects=True, vmem_limit_bytes=58 * MIB
        ),
    )(source_block, slot_block, order, rows, inverse_lower, inverse_upper, front)


def assemble_kernel(place, arrived, initial, upper, lower, out, upper_out, lower_out):
    parent = pl.program_id(0)
    block_rows = 128
    slots = arrived.shape[3] // block_rows
    upper_out[...] = upper[...]
    lower_out[...] = lower[...]

    together = 4

    def some(step, carry):
        blocks = [step * together + k for k in range(together)]
        at = [pl.ds(pl.multiple_of(b * block_rows, block_rows), block_rows) for b in blocks]
        held = []
        for b, lanes in zip(blocks, at):
            terms = [initial[0, :, lanes]]
            for child in range(2):
                source = place[parent * 2 + child, b]
                row = lax.shift_right_logical(source, 2)
                slot = lax.bitwise_and(source, slots - 1)
                slot_lanes = pl.ds(pl.multiple_of(slot * block_rows, block_rows), block_rows)
                terms.append(arrived[row, child, :, slot_lanes])
            held.append(terms)
        for lanes, (first, left, right) in zip(at, held):
            total = left.astype(jnp.float32) + right.astype(jnp.float32)
            out[0, :, lanes] = (first.astype(jnp.float32) + total).astype(jnp.bfloat16)
        return carry

    lax.fori_loop(0, out.shape[2] // block_rows // together, some, 0, unroll=2)


def assemble(place, arrived, initial, upper, lower):
    parents, piece, order = initial.shape
    rows, _, _, width = arrived.shape
    part = lambda array: pl.BlockSpec(
        (array.shape[0] // parents, array.shape[1]), lambda p: (p, 0)
    )
    return pl.pallas_call(
        assemble_kernel,
        grid=(parents,),
        out_shape=(
            jax.ShapeDtypeStruct(initial.shape, initial.dtype),
            jax.ShapeDtypeStruct(upper.shape, upper.dtype),
            jax.ShapeDtypeStruct(lower.shape, lower.dtype),
        ),
        in_specs=[
            pl.BlockSpec(memory_space=pltpu.SMEM),
            pl.BlockSpec((rows, 2, piece, width), lambda p: (0, p, 0, 0)),
            pl.BlockSpec((1, piece, order), lambda p: (p, 0, 0)),
            part(upper),
            part(lower),
        ],
        out_specs=(
            pl.BlockSpec((1, piece, order), lambda p: (p, 0, 0)),
            part(upper),
            part(lower),
        ),
        compiler_params=pltpu.CompilerParams(vmem_limit_bytes=58 * MIB),
    )(place, arrived, initial, upper, lower)


def places(slot_block, parent_map, parent_blocks):
    block_ids = jnp.arange(parent_map.shape[1], dtype=jnp.int32)
    hit = slot_block[:, :, None] == block_ids[None, None, :]
    target = jnp.sum(jnp.where(hit, parent_map[:, None, :] + 1, 0), axis=2) - 1
    parent_ids = jnp.arange(parent_blocks, dtype=jnp.int32)
    slot_ids = jnp.arange(slot_block.shape[1], dtype=jnp.int32)
    match = target[:, None, :] == parent_ids[None, :, None]
    empty = jnp.max(jnp.where(slot_block < 0, slot_ids[None, :], 0), axis=1)
    held = jnp.sum(jnp.where(match, slot_ids[None, None, :] + 1, 0), axis=2)
    return jnp.where(held > 0, held - 1, empty[:, None])


def shards(
    pivot_rows,
    pivot_order,
    inverse_lower,
    inverse_upper,
    front_rows,
    slot_block,
    parent_map,
    parent_init,
):
    rows, cols = lax.axis_size("row"), lax.axis_size("col")
    parent_blocks = parent_init.shape[2] // front_rows.shape[2]
    parent_ids = jnp.arange(parent_blocks, dtype=jnp.int32)
    block_ids = jnp.arange(parent_map.shape[1], dtype=jnp.int32)
    hits = parent_map[:, None, :] == parent_ids[None, :, None]
    source_block = jnp.sum(jnp.where(hits, block_ids[None, None, :] + 1, 0), axis=2) - 1
    upper, lower, arrived = factor_update(
        source_block,
        slot_block,
        pivot_order,
        jnp.swapaxes(pivot_rows, 1, 2),
        inverse_lower,
        inverse_upper,
        front_rows,
        rows * cols,
    )
    place = places(slot_block, parent_map, parent_blocks)
    assembled, upper, lower = assemble(
        place, arrived.reshape(rows, cols, *arrived.shape[1:]), parent_init, upper, lower
    )
    return (lower.reshape(*front_rows.shape[:3], -1), upper.T[None], assembled)


def solution(mesh):
    return jax.shard_map(
        shards,
        mesh=mesh,
        in_specs=(
            P("col", None, "row"),
            P("col", None),
            P("col", None, None),
            P("col", None, None),
            P("col", "row", None, None),
            P(),
            P(),
            P(None, ("row", "col"), None),
        ),
        out_specs=(
            P("col", "row", None, None),
            P("col", None, "row"),
            P(None, ("row", "col"), None),
        ),
        check_vma=False,
    )
```

```python
import jax
import jax.numpy as jnp
from jax import lax
from jax.experimental import pallas as pl
from jax.experimental.pallas import tpu as pltpu
from jax.sharding import PartitionSpec as P

MIB = 1024 * 1024
NT = (((1,), (1,)), ((), ()))


def column_of(row):
    count = row.shape[1]
    down = lax.broadcasted_iota(jnp.int32, (count, count), 0)
    along = lax.broadcasted_iota(jnp.int32, (count, count), 1)
    return jnp.sum(jnp.where(down == along, row, 0), axis=1, keepdims=True)


def place_row(slots, targets, width):
    count, blocks = slots.shape[1], targets.shape[1]
    block_ids = lax.broadcasted_iota(jnp.int32, (count, blocks), 1)
    hit = column_of(slots) == block_ids
    target = jnp.max(jnp.where(hit, targets, -1), axis=1, keepdims=True)
    parent_ids = lax.broadcasted_iota(jnp.int32, (count, width), 1)
    slot_ids = lax.broadcasted_iota(jnp.int32, (count, width), 0)
    held = jnp.max(jnp.where(target == parent_ids, slot_ids, -1), axis=0, keepdims=True)
    along = lax.broadcasted_iota(jnp.int32, slots.shape, 1)
    empty = jnp.max(jnp.where(slots < 0, along, 0), axis=1, keepdims=True)
    return jnp.where(held >= 0, held, empty)


def source_row(targets, width):
    blocks = targets.shape[1]
    parent_ids = lax.broadcasted_iota(jnp.int32, (blocks, width), 1)
    block_ids = lax.broadcasted_iota(jnp.int32, (blocks, width), 0)
    hit = column_of(targets) == parent_ids
    return jnp.max(jnp.where(hit, block_ids, -1), axis=0, keepdims=True)


def factor_update_exchange(
    slot_block,
    slot_rows,
    parent_map,
    order,
    rows,
    inverse_lower,
    inverse_upper,
    front,
    upper_out,
    lower_out,
    arrived,
    table_out,
    gathered,
    child,
    spread,
    chosen,
    rows_held,
    inverse_lower_held,
    inverse_upper_held,
    lead,
    lower,
    trailing,
    table,
    source,
    send_sem,
    recv_sem,
    load_sem,
    trailing_sem,
    store_sem,
    push_sem,
    land_sem,
):
    row_index = lax.axis_index("row")
    col_index = lax.axis_index("col")
    z, x = row_index // 4, lax.rem(row_index, 4)
    y, core = col_index // 2, lax.rem(col_index, 2)
    slots, block_rows, pivots = lead.shape
    width = rows_held.shape[0]
    quarter = width // 4
    pairs, pair_width = 8, 2 * width
    pair_blocks = pair_width // block_rows
    devices, piece, lanes = spread.shape

    def at_row(dz, dx):
        return lax.rem(z + dz + 4, 4) * 4 + lax.rem(x + dx + 4, 4)

    def load(source, target, sem):
        copy = pltpu.make_async_copy(source, target, sem)
        copy.start()
        return copy

    rows_in = load(rows.at[0], rows_held, load_sem.at[0])
    inverse_lower_in = load(inverse_lower.at[0], inverse_lower_held, load_sem.at[1])

    def trailing_of(pair):
        start = pivots + pair * pair_width
        return pltpu.make_async_copy(
            front.at[0, :, :, pl.ds(start, pair_width)],
            trailing.at[pair % 2],
            trailing_sem.at[pair % 2],
        )

    def partner(number):
        dz, dx = number // 32, lax.rem(number // 8, 4)
        dy, dc = lax.rem(number // 2, 4), lax.rem(number, 2)
        other_col = lax.rem(y + dy, 4) * 2 + lax.rem(core + dc, 2)
        return lax.rem(z + dz, 4) * 4 + lax.rem(x + dx, 4), other_col

    barrier = pltpu.get_barrier_semaphore()

    near = [(at_row(dz, dx), col_index) for dz, dx in ((0, 1), (0, -1), (1, 0), (-1, 0))]
    across = [(row_index, partner(number)[1]) for number in range(1, 8)]
    for other in near + across:
        pl.semaphore_signal(
            barrier, inc=1, device_id=other, device_id_type=pl.DeviceIdType.MESH
        )

    target = lax.broadcasted_iota(jnp.int32, (pivots, pivots), 0)
    chosen[...] = jnp.where(target == order[...], 1.0, 0.0).astype(jnp.bfloat16)
    rows_in.wait()
    inverse_lower_in.wait()
    lead_in = load(front.at[0, :, :, pl.ds(0, pivots)], lead, load_sem.at[2])
    inverse_upper_in = load(inverse_upper.at[0], inverse_upper_held, load_sem.at[3])
    trailing_of(0).start()
    trailing_of(1).start()

    def place(offset, part):
        start = at_row(*offset) * width + part * quarter
        return gathered.at[pl.ds(pl.multiple_of(start, 16), quarter)]

    numbers = {}
    sent = []

    def message(key, offset):
        _, part, axis, step = key
        number = numbers.setdefault(key, len(numbers))
        toward = (step, 0) if axis == 0 else (0, step)
        return pltpu.make_async_remote_copy(
            src_ref=place(offset, part),
            dst_ref=place(offset, part),
            send_sem=send_sem.at[number],
            recv_sem=recv_sem.at[number],
            device_id=(at_row(*toward), col_index),
            device_id_type=pl.DeviceIdType.MESH,
        )

    def send(offset, part, axis, step):
        seen = list(offset)
        seen[axis] -= step
        if seen[axis] == -2:
            seen[axis] = 2
        copy = message((tuple(seen), part, axis, step), offset)
        copy.start()
        sent.append(copy)

    def receive(offset, part, axis, step):
        message((offset, part, axis, step), offset).wait_recv()

    parts = ((0, 1), (2, 3))
    first = (1, 0)
    second = (0, 1)

    def offset_of(half, near, far):
        return (far, near) if half == 0 else (near, far)

    for part in (0, 2, 1, 3):
        span = pl.ds(part * quarter, quarter)
        permuted = jnp.dot(rows_held[span], chosen[...], preferred_element_type=jnp.float32)
        upper = lax.dot_general(
            permuted.astype(jnp.bfloat16),
            inverse_lower_held[...],
            NT,
            preferred_element_type=jnp.float32,
        )
        start = pl.multiple_of(row_index * width + part * quarter, 16)
        gathered[pl.ds(start, quarter)] = upper.astype(jnp.bfloat16)
        if part == 0:
            pl.semaphore_wait(barrier, len(near + across))
        half = part // 2
        for step in (1, -1):
            send((0, 0), part, first[half], step)
        for step in (1, -1):
            send((0, 0), part, second[half], step)
    own = pl.ds(pl.multiple_of(row_index * width, 16), width)
    upper_done = load(gathered.at[own], upper_out, store_sem.at[0])

    lead_in.wait()
    inverse_upper_in.wait()
    for s in range(slots):
        live = slot_block[col_index, row_index * slots + s] >= 0
        value = jnp.dot(lead[s], inverse_upper_held[...], preferred_element_type=jnp.float32)
        lower[pl.ds(s * block_rows, block_rows)] = jnp.where(live, value, 0.0).astype(jnp.bfloat16)
    lower_done = load(lower, lower_out, store_sem.at[1])

    live = [slot_block[col_index, row_index * slots + s] >= 0 for s in range(slots)]

    def turn(pair):
        trailing_of(pair).wait()

        def one(b, carry):
            columns = pl.ds(pl.multiple_of(b * block_rows, block_rows), block_rows)
            held = pl.ds((pair * pair_blocks + b) * 2, 2)
            for s in range(slots):
                turned = trailing[pair % 2, s, :, columns].T
                turned = jnp.where(live[s], turned, jnp.zeros_like(turned))
                child[held, :, pl.ds(s * block_rows, block_rows)] = turned.reshape(
                    2, piece, block_rows
                )
            return carry

        lax.fori_loop(0, pair_blocks, one, 0)
        if pair + 2 < pairs:
            trailing_of(pair + 2).start()

    def update(dz, dx):
        chunk = at_row(dz, dx)
        span = pl.ds(pl.multiple_of(chunk * width, 16), width)
        held = pl.ds(chunk * (width // piece), width // piece)
        product = lax.dot_general(
            gathered[span], lower[...], NT, preferred_element_type=jnp.float32
        ).reshape(width // piece, piece, lanes)
        child[held] = (child[held].astype(jnp.float32) - product).astype(jnp.bfloat16)

    def each():
        for k in range(2):
            for half in range(2):
                for step in (1, -1):
                    yield k, half, step, parts[half][k]

    def relay(near):
        for k, half, step, part in each():
            offset = offset_of(half, near, -step)
            receive(offset, part, second[half], step)
            if (k == 0) == (step == 1):
                send(offset, part, second[half], step)

    def finish(near):
        for k in range(2):
            for half in range(2):
                step = 1 if k == 0 else -1
                receive(offset_of(half, near, 2), parts[half][k], second[half], step)

    turn(0)
    for k, half, step, part in each():
        offset = offset_of(half, -step, 0)
        receive(offset, part, first[half], step)
        if (k == 0) == (step == 1):
            send(offset, part, first[half], step)
        for other in (1, -1):
            send(offset, part, second[half], other)
    turn(1)
    relay(0)
    turn(2)
    for k in range(2):
        for half in range(2):
            step = 1 if k == 0 else -1
            offset = offset_of(half, 2, 0)
            receive(offset, parts[half][k], first[half], step)
            for other in (1, -1):
                send(offset, parts[half][k], second[half], other)
    turn(3)
    turn(4)
    turn(5)
    relay(-1)
    turn(6)
    turn(7)
    fronts, columns = slot_rows.shape[0], table.shape[1]
    for f in range(fronts):
        table[f : f + 1] = place_row(slot_rows[f : f + 1], parent_map[f : f + 1], columns)
    own_map = parent_map[pl.ds(col_index, 1)]
    table[fronts : fronts + 1] = source_row(own_map, columns)
    table_done = load(table, table_out, store_sem.at[3])
    source_done = load(table, source, store_sem.at[4])
    relay(1)
    update(0, 0)
    for step in (1, -1):
        update(0, step)
        update(step, 0)
    finish(0)
    relay(2)
    for dz in (1, -1):
        for dx in (1, -1):
            update(dz, dx)
    update(0, 2)
    update(2, 0)
    finish(-1)
    finish(1)
    for step in (1, -1):
        update(step, 2)
        update(2, step)
    finish(2)
    update(2, 2)

    me = row_index * 8 + col_index
    source_done.wait()

    def fill(other):
        at = source[fronts, other // 2]
        value = child[jnp.maximum(at, 0) * 2 + lax.rem(other, 2)]
        spread[other] = jnp.where(at >= 0, value, jnp.zeros_like(value))

    def push(number, carry):
        other = partner(lax.rem(number * 109, devices))
        to = other[0] * 8 + other[1]
        fill(to)
        pltpu.make_async_remote_copy(
            src_ref=spread.at[to],
            dst_ref=arrived.at[me],
            send_sem=push_sem,
            recv_sem=land_sem,
            device_id=other,
            device_id_type=pl.DeviceIdType.MESH,
        ).start()
        return carry

    lax.fori_loop(1, devices, push, 0)
    fill(me)
    kept = load(spread.at[me], arrived.at[me], store_sem.at[2])
    for copy in sent:
        copy.wait_send()
    upper_done.wait()
    lower_done.wait()
    table_done.wait()
    kept.wait()
    others = pl.ds(0, devices - 1)
    pushed = pltpu.make_async_remote_copy(
        src_ref=spread.at[others],
        dst_ref=arrived.at[others],
        send_sem=push_sem,
        recv_sem=land_sem,
        device_id=partner(1),
        device_id_type=pl.DeviceIdType.MESH,
    )
    pushed.wait_send()
    pushed.wait_recv()


def factor_update(slot_block, parent_map, order, rows, inverse_lower, inverse_upper, front, devices):
    pivots = inverse_lower.shape[1]
    width = rows.shape[1]
    slots, block_rows, size = front.shape[1:]
    lanes = slots * block_rows
    piece = 64
    table = (16, 128)
    smem = pl.BlockSpec(memory_space=pltpu.SMEM)
    vmem = pl.BlockSpec(memory_space=pltpu.VMEM)
    anywhere = pl.BlockSpec(memory_space=pl.ANY)
    return pl.pallas_call(
        factor_update_exchange,
        out_shape=(
            jax.ShapeDtypeStruct((width, pivots), jnp.bfloat16),
            jax.ShapeDtypeStruct((lanes, pivots), jnp.bfloat16),
            jax.ShapeDtypeStruct((devices, piece, lanes), jnp.bfloat16),
            jax.ShapeDtypeStruct(table, jnp.int32),
        ),
        in_specs=[
            smem,
            vmem,
            vmem,
            vmem,
            anywhere,
            anywhere,
            anywhere,
            anywhere,
        ],
        out_specs=(anywhere, anywhere, anywhere, anywhere),
        scratch_shapes=[
            pltpu.VMEM((size - pivots, pivots), jnp.bfloat16),
            pltpu.VMEM(((size - pivots) // piece, piece, lanes), jnp.bfloat16),
            pltpu.VMEM((devices, piece, lanes), jnp.bfloat16),
            pltpu.VMEM((pivots, pivots), jnp.bfloat16),
            pltpu.VMEM((width, pivots), jnp.bfloat16),
            pltpu.VMEM((pivots, pivots), jnp.bfloat16),
            pltpu.VMEM((pivots, pivots), jnp.bfloat16),
            pltpu.VMEM((slots, block_rows, pivots), jnp.bfloat16),
            pltpu.VMEM((lanes, pivots), jnp.bfloat16),
            pltpu.VMEM((2, slots, block_rows, 2 * width), jnp.bfloat16),
            pltpu.VMEM(table, jnp.int32),
            pltpu.SMEM(table, jnp.int32),
            pltpu.SemaphoreType.DMA((60,)),
            pltpu.SemaphoreType.DMA((60,)),
            pltpu.SemaphoreType.DMA((4,)),
            pltpu.SemaphoreType.DMA((2,)),
            pltpu.SemaphoreType.DMA((5,)),
            pltpu.SemaphoreType.DMA,
            pltpu.SemaphoreType.DMA,
        ],
        compiler_params=pltpu.CompilerParams(
            collective_id=0, has_side_effects=True, vmem_limit_bytes=58 * MIB
        ),
    )(slot_block, slot_block, parent_map, order, rows, inverse_lower, inverse_upper, front)


def assemble_kernel(place, arrived, initial, upper, lower, out, upper_out, lower_out):
    parent = pl.program_id(0)
    block_rows = 128
    slots = arrived.shape[3] // block_rows
    upper_out[...] = upper[...]
    lower_out[...] = lower[...]

    together = 4

    def some(step, carry):
        blocks = [step * together + k for k in range(together)]
        at = [pl.ds(pl.multiple_of(b * block_rows, block_rows), block_rows) for b in blocks]
        held = []
        for b, lanes in zip(blocks, at):
            terms = [initial[0, :, lanes]]
            for child in range(2):
                source = place[parent * 2 + child, b]
                row = lax.shift_right_logical(source, 2)
                slot = lax.bitwise_and(source, slots - 1)
                slot_lanes = pl.ds(pl.multiple_of(slot * block_rows, block_rows), block_rows)
                terms.append(arrived[row, child, :, slot_lanes])
            held.append(terms)
        for lanes, (first, left, right) in zip(at, held):
            total = left.astype(jnp.float32) + right.astype(jnp.float32)
            out[0, :, lanes] = (first.astype(jnp.float32) + total).astype(jnp.bfloat16)
        return carry

    lax.fori_loop(0, out.shape[2] // block_rows // together, some, 0, unroll=2)


def assemble(place, arrived, initial, upper, lower):
    parents, piece, order = initial.shape
    rows, _, _, width = arrived.shape
    part = lambda array: pl.BlockSpec(
        (array.shape[0] // parents, array.shape[1]), lambda p: (p, 0)
    )
    return pl.pallas_call(
        assemble_kernel,
        grid=(parents,),
        out_shape=(
            jax.ShapeDtypeStruct(initial.shape, initial.dtype),
            jax.ShapeDtypeStruct(upper.shape, upper.dtype),
            jax.ShapeDtypeStruct(lower.shape, lower.dtype),
        ),
        in_specs=[
            pl.BlockSpec(memory_space=pltpu.SMEM),
            pl.BlockSpec((rows, 2, piece, width), lambda p: (0, p, 0, 0)),
            pl.BlockSpec((1, piece, order), lambda p: (p, 0, 0)),
            part(upper),
            part(lower),
        ],
        out_specs=(
            pl.BlockSpec((1, piece, order), lambda p: (p, 0, 0)),
            part(upper),
            part(lower),
        ),
        compiler_params=pltpu.CompilerParams(vmem_limit_bytes=58 * MIB),
    )(place, arrived, initial, upper, lower)


def shards(
    pivot_rows,
    pivot_order,
    inverse_lower,
    inverse_upper,
    front_rows,
    slot_block,
    parent_map,
    parent_init,
):
    rows, cols = lax.axis_size("row"), lax.axis_size("col")
    upper, lower, arrived, place = factor_update(
        slot_block,
        parent_map,
        pivot_order,
        jnp.swapaxes(pivot_rows, 1, 2),
        inverse_lower,
        inverse_upper,
        front_rows,
        rows * cols,
    )
    assembled, upper, lower = assemble(
        place, arrived.reshape(rows, cols, *arrived.shape[1:]), parent_init, upper, lower
    )
    return (lower.reshape(*front_rows.shape[:3], -1), upper.T[None], assembled)


def solution(mesh):
    return jax.shard_map(
        shards,
        mesh=mesh,
        in_specs=(
            P("col", None, "row"),
            P("col", None),
            P("col", None, None),
            P("col", None, None),
            P("col", "row", None, None),
            P(),
            P(),
            P(None, ("row", "col"), None),
        ),
        out_specs=(
            P("col", "row", None, None),
            P("col", None, "row"),
            P(None, ("row", "col"), None),
        ),
        check_vma=False,
    )
```

```python
import jax
import jax.numpy as jnp
from jax import lax
from jax.experimental import pallas as pl
from jax.experimental.pallas import tpu as pltpu
from jax.sharding import PartitionSpec as P

MIB = 1024 * 1024
NT = (((1,), (1,)), ((), ()))


def in_hbm(array):
    return pltpu.with_memory_space_constraint(array, pltpu.HBM)


def column_of(row):
    count = row.shape[1]
    down = lax.broadcasted_iota(jnp.int32, (count, count), 0)
    along = lax.broadcasted_iota(jnp.int32, (count, count), 1)
    return jnp.sum(jnp.where(down == along, row, 0), axis=1, keepdims=True)


def place_row(slots, targets, width):
    count, blocks = slots.shape[1], targets.shape[1]
    block_ids = lax.broadcasted_iota(jnp.int32, (count, blocks), 1)
    hit = column_of(slots) == block_ids
    target = jnp.max(jnp.where(hit, targets, -1), axis=1, keepdims=True)
    parent_ids = lax.broadcasted_iota(jnp.int32, (count, width), 1)
    slot_ids = lax.broadcasted_iota(jnp.int32, (count, width), 0)
    held = jnp.max(jnp.where(target == parent_ids, slot_ids, -1), axis=0, keepdims=True)
    along = lax.broadcasted_iota(jnp.int32, slots.shape, 1)
    empty = jnp.max(jnp.where(slots < 0, along, 0), axis=1, keepdims=True)
    return jnp.where(held >= 0, held, empty)


def source_row(targets, width):
    blocks = targets.shape[1]
    parent_ids = lax.broadcasted_iota(jnp.int32, (blocks, width), 1)
    block_ids = lax.broadcasted_iota(jnp.int32, (blocks, width), 0)
    hit = column_of(targets) == parent_ids
    return jnp.max(jnp.where(hit, block_ids, -1), axis=0, keepdims=True)


def factor_update_exchange(
    slot_block,
    slot_rows_in,
    parent_map_in,
    order_in,
    rows,
    inverse_lower,
    inverse_upper,
    front,
    upper_out,
    lower_out,
    arrived,
    table_out,
    gathered,
    child,
    spread,
    chosen,
    rows_held,
    inverse_lower_held,
    inverse_upper_held,
    lead,
    lower,
    trailing,
    table,
    slot_rows,
    parent_map,
    order,
    source,
    send_sem,
    recv_sem,
    load_sem,
    trailing_sem,
    store_sem,
    push_sem,
    land_sem,
):
    row_index = lax.axis_index("row")
    col_index = lax.axis_index("col")
    z, x = row_index // 4, lax.rem(row_index, 4)
    y, core = col_index // 2, lax.rem(col_index, 2)
    slots, block_rows, pivots = lead.shape
    width = rows_held.shape[0]
    quarter = width // 4
    pairs, pair_width = 8, 2 * width
    pair_blocks = pair_width // block_rows
    devices, piece, lanes = spread.shape

    def at_row(dz, dx):
        return lax.rem(z + dz + 4, 4) * 4 + lax.rem(x + dx + 4, 4)

    def load(source, target, sem):
        copy = pltpu.make_async_copy(source, target, sem)
        copy.start()
        return copy

    small = [
        load(order_in, order, load_sem.at[4]),
        load(slot_rows_in, slot_rows, load_sem.at[5]),
        load(parent_map_in, parent_map, load_sem.at[6]),
    ]
    rows_in = load(rows.at[0], rows_held, load_sem.at[0])
    inverse_lower_in = load(inverse_lower.at[0], inverse_lower_held, load_sem.at[1])

    def trailing_of(pair):
        start = pivots + pair * pair_width
        return pltpu.make_async_copy(
            front.at[0, :, :, pl.ds(start, pair_width)],
            trailing.at[pair % 2],
            trailing_sem.at[pair % 2],
        )

    def partner(number):
        dz, dx = number // 32, lax.rem(number // 8, 4)
        dy, dc = lax.rem(number // 2, 4), lax.rem(number, 2)
        other_col = lax.rem(y + dy, 4) * 2 + lax.rem(core + dc, 2)
        return lax.rem(z + dz, 4) * 4 + lax.rem(x + dx, 4), other_col

    barrier = pltpu.get_barrier_semaphore()

    near = [(at_row(dz, dx), col_index) for dz, dx in ((0, 1), (0, -1), (1, 0), (-1, 0))]
    across = [(row_index, partner(number)[1]) for number in range(1, 8)]
    for other in near + across:
        pl.semaphore_signal(
            barrier, inc=1, device_id=other, device_id_type=pl.DeviceIdType.MESH
        )

    target = lax.broadcasted_iota(jnp.int32, (pivots, pivots), 0)
    for copy in small:
        copy.wait()
    chosen[...] = jnp.where(target == order[...], 1.0, 0.0).astype(jnp.bfloat16)
    rows_in.wait()
    inverse_lower_in.wait()
    lead_in = load(front.at[0, :, :, pl.ds(0, pivots)], lead, load_sem.at[2])
    inverse_upper_in = load(inverse_upper.at[0], inverse_upper_held, load_sem.at[3])
    trailing_of(0).start()
    trailing_of(1).start()

    def place(offset, part):
        start = at_row(*offset) * width + part * quarter
        return gathered.at[pl.ds(pl.multiple_of(start, 16), quarter)]

    numbers = {}
    sent = []

    def message(key, offset):
        _, part, axis, step = key
        number = numbers.setdefault(key, len(numbers))
        toward = (step, 0) if axis == 0 else (0, step)
        return pltpu.make_async_remote_copy(
            src_ref=place(offset, part),
            dst_ref=place(offset, part),
            send_sem=send_sem.at[number],
            recv_sem=recv_sem.at[number],
            device_id=(at_row(*toward), col_index),
            device_id_type=pl.DeviceIdType.MESH,
        )

    def send(offset, part, axis, step):
        seen = list(offset)
        seen[axis] -= step
        if seen[axis] == -2:
            seen[axis] = 2
        copy = message((tuple(seen), part, axis, step), offset)
        copy.start()
        sent.append(copy)

    def receive(offset, part, axis, step):
        message((offset, part, axis, step), offset).wait_recv()

    parts = ((0, 1), (2, 3))
    first = (1, 0)
    second = (0, 1)

    def offset_of(half, near, far):
        return (far, near) if half == 0 else (near, far)

    for part in (0, 2, 1, 3):
        span = pl.ds(part * quarter, quarter)
        permuted = jnp.dot(rows_held[span], chosen[...], preferred_element_type=jnp.float32)
        upper = lax.dot_general(
            permuted.astype(jnp.bfloat16),
            inverse_lower_held[...],
            NT,
            preferred_element_type=jnp.float32,
        )
        start = pl.multiple_of(row_index * width + part * quarter, 16)
        gathered[pl.ds(start, quarter)] = upper.astype(jnp.bfloat16)
        if part == 0:
            pl.semaphore_wait(barrier, len(near + across))
        half = part // 2
        for step in (1, -1):
            send((0, 0), part, first[half], step)
        for step in (1, -1):
            send((0, 0), part, second[half], step)
    own = pl.ds(pl.multiple_of(row_index * width, 16), width)
    upper_done = load(gathered.at[own], upper_out, store_sem.at[0])

    lead_in.wait()
    inverse_upper_in.wait()
    for s in range(slots):
        live = slot_block[col_index, row_index * slots + s] >= 0
        value = jnp.dot(lead[s], inverse_upper_held[...], preferred_element_type=jnp.float32)
        lower[pl.ds(s * block_rows, block_rows)] = jnp.where(live, value, 0.0).astype(jnp.bfloat16)
    lower_done = load(lower, lower_out, store_sem.at[1])

    live = [slot_block[col_index, row_index * slots + s] >= 0 for s in range(slots)]

    def turn(pair):
        trailing_of(pair).wait()

        def one(b, carry):
            columns = pl.ds(pl.multiple_of(b * block_rows, block_rows), block_rows)
            held = pl.ds((pair * pair_blocks + b) * 2, 2)
            for s in range(slots):
                turned = trailing[pair % 2, s, :, columns].T
                turned = jnp.where(live[s], turned, jnp.zeros_like(turned))
                child[held, :, pl.ds(s * block_rows, block_rows)] = turned.reshape(
                    2, piece, block_rows
                )
            return carry

        lax.fori_loop(0, pair_blocks, one, 0)
        if pair + 2 < pairs:
            trailing_of(pair + 2).start()

    def update(dz, dx):
        chunk = at_row(dz, dx)
        span = pl.ds(pl.multiple_of(chunk * width, 16), width)
        held = pl.ds(chunk * (width // piece), width // piece)
        product = lax.dot_general(
            gathered[span], lower[...], NT, preferred_element_type=jnp.float32
        ).reshape(width // piece, piece, lanes)
        child[held] = (child[held].astype(jnp.float32) - product).astype(jnp.bfloat16)

    def each():
        for k in range(2):
            for half in range(2):
                for step in (1, -1):
                    yield k, half, step, parts[half][k]

    def relay(near):
        for k, half, step, part in each():
            offset = offset_of(half, near, -step)
            receive(offset, part, second[half], step)
            if (k == 0) == (step == 1):
                send(offset, part, second[half], step)

    def finish(near):
        for k in range(2):
            for half in range(2):
                step = 1 if k == 0 else -1
                receive(offset_of(half, near, 2), parts[half][k], second[half], step)

    turn(0)
    for k, half, step, part in each():
        offset = offset_of(half, -step, 0)
        receive(offset, part, first[half], step)
        if (k == 0) == (step == 1):
            send(offset, part, first[half], step)
        for other in (1, -1):
            send(offset, part, second[half], other)
    turn(1)
    relay(0)
    turn(2)
    for k in range(2):
        for half in range(2):
            step = 1 if k == 0 else -1
            offset = offset_of(half, 2, 0)
            receive(offset, parts[half][k], first[half], step)
            for other in (1, -1):
                send(offset, parts[half][k], second[half], other)
    turn(3)
    turn(4)
    turn(5)
    relay(-1)
    turn(6)
    turn(7)
    fronts, columns = slot_rows.shape[0], table.shape[1]
    for f in range(fronts):
        table[f : f + 1] = place_row(slot_rows[f : f + 1], parent_map[f : f + 1], columns)
    own_map = parent_map[pl.ds(col_index, 1)]
    table[fronts : fronts + 1] = source_row(own_map, columns)
    table_done = load(table, table_out, store_sem.at[3])
    source_done = load(table, source, store_sem.at[4])
    relay(1)
    update(0, 0)
    for step in (1, -1):
        update(0, step)
        update(step, 0)
    finish(0)
    relay(2)
    for dz in (1, -1):
        for dx in (1, -1):
            update(dz, dx)
    update(0, 2)
    update(2, 0)
    finish(-1)
    finish(1)
    for step in (1, -1):
        update(step, 2)
        update(2, step)
    finish(2)
    update(2, 2)

    me = row_index * 8 + col_index
    source_done.wait()

    def fill(other):
        at = source[fronts, other // 2]
        value = child[jnp.maximum(at, 0) * 2 + lax.rem(other, 2)]
        spread[other] = jnp.where(at >= 0, value, jnp.zeros_like(value))

    def push(number, carry):
        other = partner(lax.rem(number * 109, devices))
        to = other[0] * 8 + other[1]
        fill(to)
        pltpu.make_async_remote_copy(
            src_ref=spread.at[to],
            dst_ref=arrived.at[me],
            send_sem=push_sem,
            recv_sem=land_sem,
            device_id=other,
            device_id_type=pl.DeviceIdType.MESH,
        ).start()
        return carry

    lax.fori_loop(1, devices, push, 0)
    fill(me)
    kept = load(spread.at[me], arrived.at[me], store_sem.at[2])
    for copy in sent:
        copy.wait_send()
    upper_done.wait()
    lower_done.wait()
    table_done.wait()
    kept.wait()
    others = pl.ds(0, devices - 1)
    pushed = pltpu.make_async_remote_copy(
        src_ref=spread.at[others],
        dst_ref=arrived.at[others],
        send_sem=push_sem,
        recv_sem=land_sem,
        device_id=partner(1),
        device_id_type=pl.DeviceIdType.MESH,
    )
    pushed.wait_send()
    pushed.wait_recv()


def factor_update(slot_block, parent_map, order, rows, inverse_lower, inverse_upper, front, devices):
    pivots = inverse_lower.shape[1]
    width = rows.shape[1]
    slots, block_rows, size = front.shape[1:]
    lanes = slots * block_rows
    piece = 64
    table = (16, 128)
    smem = pl.BlockSpec(memory_space=pltpu.SMEM)
    anywhere = pl.BlockSpec(memory_space=pl.ANY)
    operands = (slot_block, parent_map, order, rows, inverse_lower, inverse_upper, front)
    return pl.pallas_call(
        factor_update_exchange,
        out_shape=(
            jax.ShapeDtypeStruct((width, pivots), jnp.bfloat16),
            jax.ShapeDtypeStruct((lanes, pivots), jnp.bfloat16),
            pltpu.VMEM((devices, piece, lanes), jnp.bfloat16),
            jax.ShapeDtypeStruct(table, jnp.int32),
        ),
        in_specs=[
            smem,
            anywhere,
            anywhere,
            anywhere,
            anywhere,
            anywhere,
            anywhere,
            anywhere,
        ],
        out_specs=(
            anywhere,
            anywhere,
            pl.BlockSpec(memory_space=pltpu.VMEM),
            anywhere,
        ),
        scratch_shapes=[
            pltpu.VMEM((size - pivots, pivots), jnp.bfloat16),
            pltpu.VMEM(((size - pivots) // piece, piece, lanes), jnp.bfloat16),
            pltpu.VMEM((devices, piece, lanes), jnp.bfloat16),
            pltpu.VMEM((pivots, pivots), jnp.bfloat16),
            pltpu.VMEM((width, pivots), jnp.bfloat16),
            pltpu.VMEM((pivots, pivots), jnp.bfloat16),
            pltpu.VMEM((pivots, pivots), jnp.bfloat16),
            pltpu.VMEM((slots, block_rows, pivots), jnp.bfloat16),
            pltpu.VMEM((lanes, pivots), jnp.bfloat16),
            pltpu.VMEM((2, slots, block_rows, 2 * width), jnp.bfloat16),
            pltpu.VMEM(table, jnp.int32),
            pltpu.VMEM(slot_block.shape, jnp.int32),
            pltpu.VMEM(parent_map.shape, jnp.int32),
            pltpu.VMEM(order.shape, jnp.int32),
            pltpu.SMEM(table, jnp.int32),
            pltpu.SemaphoreType.DMA((60,)),
            pltpu.SemaphoreType.DMA((60,)),
            pltpu.SemaphoreType.DMA((7,)),
            pltpu.SemaphoreType.DMA((2,)),
            pltpu.SemaphoreType.DMA((5,)),
            pltpu.SemaphoreType.DMA,
            pltpu.SemaphoreType.DMA,
        ],
        compiler_params=pltpu.CompilerParams(
            collective_id=0, has_side_effects=True, vmem_limit_bytes=43 * MIB
        ),
    )(slot_block, *map(in_hbm, operands))


def assemble_kernel(
    place,
    arrived,
    initial,
    upper,
    lower,
    out,
    upper_out,
    lower_out,
    total,
    store_sem,
):
    parents, _, order = initial.shape
    block_rows = 128
    slots = arrived.shape[3] // block_rows
    stores = [
        pltpu.make_async_copy(upper, upper_out, store_sem.at[parents]),
        pltpu.make_async_copy(lower, lower_out, store_sem.at[parents + 1]),
    ]
    for copy in stores:
        copy.start()
    together = 4
    for parent in range(parents):

        def some(step, carry):
            blocks = [step * together + k for k in range(together)]
            at = [pl.ds(pl.multiple_of(b * block_rows, block_rows), block_rows) for b in blocks]
            terms = []
            for b, lanes in zip(blocks, at):
                term = [initial[parent, :, lanes]]
                for child in range(2):
                    source = place[parent * 2 + child, b]
                    row = lax.shift_right_logical(source, 2)
                    slot = lax.bitwise_and(source, slots - 1)
                    slot_lanes = pl.ds(pl.multiple_of(slot * block_rows, block_rows), block_rows)
                    term.append(arrived[row, 2 * parent + child, :, slot_lanes])
                terms.append(term)
            for lanes, (first, left, right) in zip(at, terms):
                both = left.astype(jnp.float32) + right.astype(jnp.float32)
                total[parent, :, lanes] = (first.astype(jnp.float32) + both).astype(jnp.bfloat16)
            return carry

        lax.fori_loop(0, order // block_rows // together, some, 0, unroll=2)
        store = pltpu.make_async_copy(total.at[parent], out.at[parent], store_sem.at[parent])
        store.start()
        stores.append(store)
    for copy in stores:
        copy.wait()


def assemble(place, arrived, initial, upper, lower):
    parents = initial.shape[0]
    anywhere = pl.BlockSpec(memory_space=pl.ANY)
    vmem = pl.BlockSpec(memory_space=pltpu.VMEM)
    return pl.pallas_call(
        assemble_kernel,
        out_shape=(
            jax.ShapeDtypeStruct(initial.shape, initial.dtype),
            jax.ShapeDtypeStruct(upper.shape, upper.dtype),
            jax.ShapeDtypeStruct(lower.shape, lower.dtype),
        ),
        in_specs=[pl.BlockSpec(memory_space=pltpu.SMEM), vmem, vmem, vmem, vmem],
        out_specs=(anywhere, anywhere, anywhere),
        scratch_shapes=[
            pltpu.VMEM(initial.shape, initial.dtype),
            pltpu.SemaphoreType.DMA((parents + 2,)),
        ],
        compiler_params=pltpu.CompilerParams(vmem_limit_bytes=8 * MIB),
    )(place, arrived, initial, upper, lower)


def shards(
    pivot_rows,
    pivot_order,
    inverse_lower,
    inverse_upper,
    front_rows,
    slot_block,
    parent_map,
    parent_init,
):
    rows, cols = lax.axis_size("row"), lax.axis_size("col")
    upper, lower, arrived, place = factor_update(
        slot_block,
        parent_map,
        pivot_order,
        jnp.swapaxes(pivot_rows, 1, 2),
        inverse_lower,
        inverse_upper,
        front_rows,
        rows * cols,
    )
    assembled, upper, lower = assemble(
        place, arrived.reshape(rows, cols, *arrived.shape[1:]), parent_init, upper, lower
    )
    return (lower.reshape(*front_rows.shape[:3], -1), upper.T[None], assembled)


def solution(mesh):
    return jax.shard_map(
        shards,
        mesh=mesh,
        in_specs=(
            P("col", None, "row"),
            P("col", None),
            P("col", None, None),
            P("col", None, None),
            P("col", "row", None, None),
            P(),
            P(),
            P(None, ("row", "col"), None),
        ),
        out_specs=(
            P("col", "row", None, None),
            P("col", None, "row"),
            P(None, ("row", "col"), None),
        ),
        check_vma=False,
    )
```

```python
import jax
import jax.numpy as jnp
from jax import lax
from jax.experimental import pallas as pl
from jax.experimental.pallas import tpu as pltpu
from jax.sharding import PartitionSpec as P

MIB = 1024 * 1024
NT = (((1,), (1,)), ((), ()))


def in_hbm(array):
    return pltpu.with_memory_space_constraint(array, pltpu.HBM)


def column_of(row):
    count = row.shape[1]
    down = lax.broadcasted_iota(jnp.int32, (count, count), 0)
    along = lax.broadcasted_iota(jnp.int32, (count, count), 1)
    return jnp.sum(jnp.where(down == along, row, 0), axis=1, keepdims=True)


def place_row(slots, targets, width):
    count, blocks = slots.shape[1], targets.shape[1]
    block_ids = lax.broadcasted_iota(jnp.int32, (count, blocks), 1)
    hit = column_of(slots) == block_ids
    target = jnp.max(jnp.where(hit, targets, -1), axis=1, keepdims=True)
    parent_ids = lax.broadcasted_iota(jnp.int32, (count, width), 1)
    slot_ids = lax.broadcasted_iota(jnp.int32, (count, width), 0)
    held = jnp.max(jnp.where(target == parent_ids, slot_ids, -1), axis=0, keepdims=True)
    along = lax.broadcasted_iota(jnp.int32, slots.shape, 1)
    empty = jnp.max(jnp.where(slots < 0, along, 0), axis=1, keepdims=True)
    return jnp.where(held >= 0, held, empty)


def source_row(targets, width):
    blocks = targets.shape[1]
    parent_ids = lax.broadcasted_iota(jnp.int32, (blocks, width), 1)
    block_ids = lax.broadcasted_iota(jnp.int32, (blocks, width), 0)
    hit = column_of(targets) == parent_ids
    return jnp.max(jnp.where(hit, block_ids, -1), axis=0, keepdims=True)


def factor_update_exchange(
    slot_block,
    slot_rows_in,
    parent_map_in,
    order_in,
    rows,
    inverse_lower,
    inverse_upper,
    front,
    upper_out,
    lower_out,
    arrived,
    table_out,
    gathered,
    child,
    spread,
    chosen,
    rows_held,
    inverse_lower_held,
    inverse_upper_held,
    lead,
    lower,
    trailing,
    table,
    slot_rows,
    parent_map,
    order,
    source,
    send_sem,
    recv_sem,
    load_sem,
    trailing_sem,
    store_sem,
    push_sem,
    land_sem,
):
    row_index = lax.axis_index("row")
    col_index = lax.axis_index("col")
    z, x = row_index // 4, lax.rem(row_index, 4)
    y, core = col_index // 2, lax.rem(col_index, 2)
    slots, block_rows, pivots = lead.shape
    width = rows_held.shape[0]
    quarter = width // 4
    pairs, pair_width = 8, 2 * width
    pair_blocks = pair_width // block_rows
    devices, piece, lanes = spread.shape

    def at_row(dz, dx):
        return lax.rem(z + dz + 4, 4) * 4 + lax.rem(x + dx + 4, 4)

    def load(source, target, sem):
        copy = pltpu.make_async_copy(source, target, sem)
        copy.start()
        return copy

    small = [
        load(order_in, order, load_sem.at[4]),
        load(slot_rows_in, slot_rows, load_sem.at[5]),
        load(parent_map_in, parent_map, load_sem.at[6]),
    ]
    rows_in = load(rows.at[0], rows_held, load_sem.at[0])
    inverse_lower_in = load(inverse_lower.at[0], inverse_lower_held, load_sem.at[1])

    def trailing_of(pair):
        start = pivots + pair * pair_width
        return pltpu.make_async_copy(
            front.at[0, :, :, pl.ds(start, pair_width)],
            trailing.at[pair % 2],
            trailing_sem.at[pair % 2],
        )

    def partner(number):
        dz, dx = number // 32, lax.rem(number // 8, 4)
        dy, dc = lax.rem(number // 2, 4), lax.rem(number, 2)
        other_col = lax.rem(y + dy, 4) * 2 + lax.rem(core + dc, 2)
        return lax.rem(z + dz, 4) * 4 + lax.rem(x + dx, 4), other_col

    barrier = pltpu.get_barrier_semaphore()

    near = [(at_row(dz, dx), col_index) for dz, dx in ((0, 1), (0, -1), (1, 0), (-1, 0))]
    across = [(row_index, partner(number)[1]) for number in range(1, 8)]
    for other in near + across:
        pl.semaphore_signal(
            barrier, inc=1, device_id=other, device_id_type=pl.DeviceIdType.MESH
        )

    target = lax.broadcasted_iota(jnp.int32, (pivots, pivots), 0)
    for copy in small:
        copy.wait()
    chosen[...] = jnp.where(target == order[...], 1.0, 0.0).astype(jnp.bfloat16)
    rows_in.wait()
    inverse_lower_in.wait()
    lead_in = load(front.at[0, :, :, pl.ds(0, pivots)], lead, load_sem.at[2])
    inverse_upper_in = load(inverse_upper.at[0], inverse_upper_held, load_sem.at[3])
    trailing_of(0).start()
    trailing_of(1).start()

    def place(offset, part):
        start = at_row(*offset) * width + part * quarter
        return gathered.at[pl.ds(pl.multiple_of(start, 16), quarter)]

    numbers = {}
    sent = []

    def message(key, offset):
        _, part, axis, step = key
        number = numbers.setdefault(key, len(numbers))
        toward = (step, 0) if axis == 0 else (0, step)
        return pltpu.make_async_remote_copy(
            src_ref=place(offset, part),
            dst_ref=place(offset, part),
            send_sem=send_sem.at[number],
            recv_sem=recv_sem.at[number],
            device_id=(at_row(*toward), col_index),
            device_id_type=pl.DeviceIdType.MESH,
        )

    def send(offset, part, axis, step):
        seen = list(offset)
        seen[axis] -= step
        if seen[axis] == -2:
            seen[axis] = 2
        copy = message((tuple(seen), part, axis, step), offset)
        copy.start()
        sent.append(copy)

    def receive(offset, part, axis, step):
        message((offset, part, axis, step), offset).wait_recv()

    parts = ((0, 1), (2, 3))
    first = (1, 0)
    second = (0, 1)

    def offset_of(half, near, far):
        return (far, near) if half == 0 else (near, far)

    for part in (0, 2, 1, 3):
        span = pl.ds(part * quarter, quarter)
        permuted = jnp.dot(rows_held[span], chosen[...], preferred_element_type=jnp.float32)
        upper = lax.dot_general(
            permuted.astype(jnp.bfloat16),
            inverse_lower_held[...],
            NT,
            preferred_element_type=jnp.float32,
        )
        start = pl.multiple_of(row_index * width + part * quarter, 16)
        gathered[pl.ds(start, quarter)] = upper.astype(jnp.bfloat16)
        if part == 0:
            pl.semaphore_wait(barrier, len(near + across))
        half = part // 2
        for step in (1, -1):
            send((0, 0), part, first[half], step)
        for step in (1, -1):
            send((0, 0), part, second[half], step)
    own = pl.ds(pl.multiple_of(row_index * width, 16), width)
    upper_done = load(gathered.at[own], upper_out, store_sem.at[0])

    lead_in.wait()
    inverse_upper_in.wait()
    for s in range(slots):
        live = slot_block[col_index, row_index * slots + s] >= 0
        value = jnp.dot(lead[s], inverse_upper_held[...], preferred_element_type=jnp.float32)
        lower[pl.ds(s * block_rows, block_rows)] = jnp.where(live, value, 0.0).astype(jnp.bfloat16)
    lower_done = load(lower, lower_out, store_sem.at[1])

    live = [slot_block[col_index, row_index * slots + s] >= 0 for s in range(slots)]

    def turn(pair):
        trailing_of(pair).wait()

        def one(b, carry):
            columns = pl.ds(pl.multiple_of(b * block_rows, block_rows), block_rows)
            held = pl.ds((pair * pair_blocks + b) * 2, 2)
            for s in range(slots):
                turned = trailing[pair % 2, s, :, columns].T
                turned = jnp.where(live[s], turned, jnp.zeros_like(turned))
                child[held, :, pl.ds(s * block_rows, block_rows)] = turned.reshape(
                    2, piece, block_rows
                )
            return carry

        lax.fori_loop(0, pair_blocks, one, 0)
        if pair + 2 < pairs:
            trailing_of(pair + 2).start()

    def update(dz, dx):
        chunk = at_row(dz, dx)
        span = pl.ds(pl.multiple_of(chunk * width, 16), width)
        held = pl.ds(chunk * (width // piece), width // piece)
        product = lax.dot_general(
            gathered[span], lower[...], NT, preferred_element_type=jnp.float32
        ).reshape(width // piece, piece, lanes)
        child[held] = (child[held].astype(jnp.float32) - product).astype(jnp.bfloat16)

    def each():
        for k in range(2):
            for half in range(2):
                for step in (1, -1):
                    yield k, half, step, parts[half][k]

    def relay(near):
        for k, half, step, part in each():
            offset = offset_of(half, near, -step)
            receive(offset, part, second[half], step)
            if (k == 0) == (step == 1):
                send(offset, part, second[half], step)

    def finish(near):
        for k in range(2):
            for half in range(2):
                step = 1 if k == 0 else -1
                receive(offset_of(half, near, 2), parts[half][k], second[half], step)

    turn(0)
    for k, half, step, part in each():
        offset = offset_of(half, -step, 0)
        receive(offset, part, first[half], step)
        if (k == 0) == (step == 1):
            send(offset, part, first[half], step)
        for other in (1, -1):
            send(offset, part, second[half], other)
    turn(1)
    relay(0)
    turn(2)
    for k in range(2):
        for half in range(2):
            step = 1 if k == 0 else -1
            offset = offset_of(half, 2, 0)
            receive(offset, parts[half][k], first[half], step)
            for other in (1, -1):
                send(offset, parts[half][k], second[half], other)
    turn(3)
    turn(4)
    turn(5)
    relay(-1)
    turn(6)
    turn(7)
    fronts, columns = slot_rows.shape[0], table.shape[1]
    for f in range(fronts):
        table[f : f + 1] = place_row(slot_rows[f : f + 1], parent_map[f : f + 1], columns)
    own_map = parent_map[pl.ds(col_index, 1)]
    table[fronts : fronts + 1] = source_row(own_map, columns)
    table_done = load(table, table_out, store_sem.at[3])
    source_done = load(table, source, store_sem.at[4])
    relay(1)
    update(0, 0)
    for step in (1, -1):
        update(0, step)
        update(step, 0)
    finish(0)
    relay(2)
    for dz in (1, -1):
        for dx in (1, -1):
            update(dz, dx)
    update(0, 2)
    update(2, 0)
    finish(-1)
    finish(1)
    for step in (1, -1):
        update(step, 2)
        update(2, step)
    finish(2)
    update(2, 2)

    me = row_index * 8 + col_index
    source_done.wait()

    def fill(other):
        at = source[fronts, other // 2]
        value = child[jnp.maximum(at, 0) * 2 + lax.rem(other, 2)]
        spread[other] = jnp.where(at >= 0, value, jnp.zeros_like(value))

    def push(number, carry):
        other = partner(lax.rem(number * 101, devices))
        to = other[0] * 8 + other[1]
        fill(to)
        pltpu.make_async_remote_copy(
            src_ref=spread.at[to],
            dst_ref=arrived.at[me],
            send_sem=push_sem,
            recv_sem=land_sem,
            device_id=other,
            device_id_type=pl.DeviceIdType.MESH,
        ).start()
        return carry

    lax.fori_loop(1, devices, push, 0)
    fill(me)
    kept = load(spread.at[me], arrived.at[me], store_sem.at[2])
    for copy in sent:
        copy.wait_send()
    upper_done.wait()
    lower_done.wait()
    table_done.wait()
    kept.wait()
    others = pl.ds(0, devices - 1)
    pushed = pltpu.make_async_remote_copy(
        src_ref=spread.at[others],
        dst_ref=arrived.at[others],
        send_sem=push_sem,
        recv_sem=land_sem,
        device_id=partner(1),
        device_id_type=pl.DeviceIdType.MESH,
    )
    pushed.wait_send()
    pushed.wait_recv()


def factor_update(slot_block, parent_map, order, rows, inverse_lower, inverse_upper, front, devices):
    pivots = inverse_lower.shape[1]
    width = rows.shape[1]
    slots, block_rows, size = front.shape[1:]
    lanes = slots * block_rows
    piece = 64
    table = (16, 128)
    smem = pl.BlockSpec(memory_space=pltpu.SMEM)
    anywhere = pl.BlockSpec(memory_space=pl.ANY)
    operands = (slot_block, parent_map, order, rows, inverse_lower, inverse_upper, front)
    return pl.pallas_call(
        factor_update_exchange,
        out_shape=(
            jax.ShapeDtypeStruct((width, pivots), jnp.bfloat16),
            jax.ShapeDtypeStruct((lanes, pivots), jnp.bfloat16),
            pltpu.VMEM((devices, piece, lanes), jnp.bfloat16),
            jax.ShapeDtypeStruct(table, jnp.int32),
        ),
        in_specs=[
            smem,
            anywhere,
            anywhere,
            anywhere,
            anywhere,
            anywhere,
            anywhere,
            anywhere,
        ],
        out_specs=(
            anywhere,
            anywhere,
            pl.BlockSpec(memory_space=pltpu.VMEM),
            anywhere,
        ),
        scratch_shapes=[
            pltpu.VMEM((size - pivots, pivots), jnp.bfloat16),
            pltpu.VMEM(((size - pivots) // piece, piece, lanes), jnp.bfloat16),
            pltpu.VMEM((devices, piece, lanes), jnp.bfloat16),
            pltpu.VMEM((pivots, pivots), jnp.bfloat16),
            pltpu.VMEM((width, pivots), jnp.bfloat16),
            pltpu.VMEM((pivots, pivots), jnp.bfloat16),
            pltpu.VMEM((pivots, pivots), jnp.bfloat16),
            pltpu.VMEM((slots, block_rows, pivots), jnp.bfloat16),
            pltpu.VMEM((lanes, pivots), jnp.bfloat16),
            pltpu.VMEM((2, slots, block_rows, 2 * width), jnp.bfloat16),
            pltpu.VMEM(table, jnp.int32),
            pltpu.VMEM(slot_block.shape, jnp.int32),
            pltpu.VMEM(parent_map.shape, jnp.int32),
            pltpu.VMEM(order.shape, jnp.int32),
            pltpu.SMEM(table, jnp.int32),
            pltpu.SemaphoreType.DMA((60,)),
            pltpu.SemaphoreType.DMA((60,)),
            pltpu.SemaphoreType.DMA((7,)),
            pltpu.SemaphoreType.DMA((2,)),
            pltpu.SemaphoreType.DMA((5,)),
            pltpu.SemaphoreType.DMA,
            pltpu.SemaphoreType.DMA,
        ],
        compiler_params=pltpu.CompilerParams(
            collective_id=0, has_side_effects=True, vmem_limit_bytes=43 * MIB
        ),
    )(slot_block, *map(in_hbm, operands))


def assemble_kernel(
    place,
    arrived,
    initial,
    upper,
    lower,
    out,
    upper_out,
    lower_out,
    total,
    store_sem,
):
    parents, _, order = initial.shape
    block_rows = 128
    slots = arrived.shape[3] // block_rows
    stores = [
        pltpu.make_async_copy(upper, upper_out, store_sem.at[parents]),
        pltpu.make_async_copy(lower, lower_out, store_sem.at[parents + 1]),
    ]
    for copy in stores:
        copy.start()
    together = 4
    for parent in range(parents):

        def some(step, carry):
            blocks = [step * together + k for k in range(together)]
            at = [pl.ds(pl.multiple_of(b * block_rows, block_rows), block_rows) for b in blocks]
            terms = []
            for b, lanes in zip(blocks, at):
                term = [initial[parent, :, lanes]]
                for child in range(2):
                    source = place[parent * 2 + child, b]
                    row = lax.shift_right_logical(source, 2)
                    slot = lax.bitwise_and(source, slots - 1)
                    slot_lanes = pl.ds(pl.multiple_of(slot * block_rows, block_rows), block_rows)
                    term.append(arrived[row, 2 * parent + child, :, slot_lanes])
                terms.append(term)
            for lanes, (first, left, right) in zip(at, terms):
                both = left.astype(jnp.float32) + right.astype(jnp.float32)
                total[parent, :, lanes] = (first.astype(jnp.float32) + both).astype(jnp.bfloat16)
            return carry

        lax.fori_loop(0, order // block_rows // together, some, 0, unroll=2)
        store = pltpu.make_async_copy(total.at[parent], out.at[parent], store_sem.at[parent])
        store.start()
        stores.append(store)
    for copy in stores:
        copy.wait()


def assemble(place, arrived, initial, upper, lower):
    parents = initial.shape[0]
    anywhere = pl.BlockSpec(memory_space=pl.ANY)
    vmem = pl.BlockSpec(memory_space=pltpu.VMEM)
    return pl.pallas_call(
        assemble_kernel,
        out_shape=(
            jax.ShapeDtypeStruct(initial.shape, initial.dtype),
            jax.ShapeDtypeStruct(upper.shape, upper.dtype),
            jax.ShapeDtypeStruct(lower.shape, lower.dtype),
        ),
        in_specs=[pl.BlockSpec(memory_space=pltpu.SMEM), vmem, vmem, vmem, vmem],
        out_specs=(anywhere, anywhere, anywhere),
        scratch_shapes=[
            pltpu.VMEM(initial.shape, initial.dtype),
            pltpu.SemaphoreType.DMA((parents + 2,)),
        ],
        compiler_params=pltpu.CompilerParams(vmem_limit_bytes=8 * MIB),
    )(place, arrived, initial, upper, lower)


def shards(
    pivot_rows,
    pivot_order,
    inverse_lower,
    inverse_upper,
    front_rows,
    slot_block,
    parent_map,
    parent_init,
):
    rows, cols = lax.axis_size("row"), lax.axis_size("col")
    upper, lower, arrived, place = factor_update(
        slot_block,
        parent_map,
        pivot_order,
        jnp.swapaxes(pivot_rows, 1, 2),
        inverse_lower,
        inverse_upper,
        front_rows,
        rows * cols,
    )
    assembled, upper, lower = assemble(
        place, arrived.reshape(rows, cols, *arrived.shape[1:]), parent_init, upper, lower
    )
    return (lower.reshape(*front_rows.shape[:3], -1), upper.T[None], assembled)


def solution(mesh):
    return jax.shard_map(
        shards,
        mesh=mesh,
        in_specs=(
            P("col", None, "row"),
            P("col", None),
            P("col", None, None),
            P("col", None, None),
            P("col", "row", None, None),
            P(),
            P(),
            P(None, ("row", "col"), None),
        ),
        out_specs=(
            P("col", "row", None, None),
            P("col", None, "row"),
            P(None, ("row", "col"), None),
        ),
        check_vma=False,
    )
```

```python
import jax
import jax.numpy as jnp
from jax import lax
from jax.experimental import pallas as pl
from jax.experimental.pallas import tpu as pltpu
from jax.sharding import PartitionSpec as P

MIB = 1024 * 1024
NT = (((1,), (1,)), ((), ()))


def in_hbm(array):
    return pltpu.with_memory_space_constraint(array, pltpu.HBM)


def column_of(row):
    count = row.shape[1]
    down = lax.broadcasted_iota(jnp.int32, (count, count), 0)
    along = lax.broadcasted_iota(jnp.int32, (count, count), 1)
    return jnp.sum(jnp.where(down == along, row, 0), axis=1, keepdims=True)


def place_row(slots, targets, width):
    count, blocks = slots.shape[1], targets.shape[1]
    block_ids = lax.broadcasted_iota(jnp.int32, (count, blocks), 1)
    hit = column_of(slots) == block_ids
    target = jnp.max(jnp.where(hit, targets, -1), axis=1, keepdims=True)
    parent_ids = lax.broadcasted_iota(jnp.int32, (count, width), 1)
    slot_ids = lax.broadcasted_iota(jnp.int32, (count, width), 0)
    held = jnp.max(jnp.where(target == parent_ids, slot_ids, -1), axis=0, keepdims=True)
    along = lax.broadcasted_iota(jnp.int32, slots.shape, 1)
    empty = jnp.max(jnp.where(slots < 0, along, 0), axis=1, keepdims=True)
    return jnp.where(held >= 0, held, empty)


def source_row(targets, width):
    blocks = targets.shape[1]
    parent_ids = lax.broadcasted_iota(jnp.int32, (blocks, width), 1)
    block_ids = lax.broadcasted_iota(jnp.int32, (blocks, width), 0)
    hit = column_of(targets) == parent_ids
    return jnp.max(jnp.where(hit, block_ids, -1), axis=0, keepdims=True)


def factor_update_exchange(
    slot_block,
    slot_rows_in,
    parent_map_in,
    order_in,
    rows,
    inverse_lower,
    inverse_upper,
    front,
    upper_out,
    lower_out,
    arrived,
    table_out,
    gathered,
    child,
    spread,
    chosen,
    rows_held,
    inverse_lower_held,
    inverse_upper_held,
    lead,
    lower,
    trailing,
    table,
    slot_rows,
    parent_map,
    order,
    source,
    send_sem,
    recv_sem,
    load_sem,
    trailing_sem,
    store_sem,
    push_sem,
    land_sem,
):
    row_index = lax.axis_index("row")
    col_index = lax.axis_index("col")
    z, x = row_index // 4, lax.rem(row_index, 4)
    y, core = col_index // 2, lax.rem(col_index, 2)
    slots, block_rows, pivots = lead.shape
    width = rows_held.shape[0]
    quarter = width // 4
    pairs, pair_width = 8, 2 * width
    pair_blocks = pair_width // block_rows
    devices, piece, lanes = spread.shape

    def at_row(dz, dx):
        return lax.rem(z + dz + 4, 4) * 4 + lax.rem(x + dx + 4, 4)

    def load(source, target, sem):
        copy = pltpu.make_async_copy(source, target, sem)
        copy.start()
        return copy

    small = [
        load(order_in, order, load_sem.at[4]),
        load(slot_rows_in, slot_rows, load_sem.at[5]),
        load(parent_map_in, parent_map, load_sem.at[6]),
    ]
    rows_in = load(rows.at[0], rows_held, load_sem.at[0])
    inverse_lower_in = load(inverse_lower.at[0], inverse_lower_held, load_sem.at[1])

    def trailing_of(pair):
        start = pivots + pair * pair_width
        return pltpu.make_async_copy(
            front.at[0, :, :, pl.ds(start, pair_width)],
            trailing.at[pair % 2],
            trailing_sem.at[pair % 2],
        )

    def partner(number):
        dz, dx = number // 32, lax.rem(number // 8, 4)
        dy, dc = lax.rem(number // 2, 4), lax.rem(number, 2)
        other_col = lax.rem(y + dy, 4) * 2 + lax.rem(core + dc, 2)
        return lax.rem(z + dz, 4) * 4 + lax.rem(x + dx, 4), other_col

    barrier = pltpu.get_barrier_semaphore()

    near = [(at_row(dz, dx), col_index) for dz, dx in ((0, 1), (0, -1), (1, 0), (-1, 0))]
    across = [(row_index, partner(number)[1]) for number in range(1, 8)]
    for other in near + across:
        pl.semaphore_signal(
            barrier, inc=1, device_id=other, device_id_type=pl.DeviceIdType.MESH
        )

    target = lax.broadcasted_iota(jnp.int32, (pivots, pivots), 0)
    for copy in small:
        copy.wait()
    chosen[...] = jnp.where(target == order[...], 1.0, 0.0).astype(jnp.bfloat16)
    rows_in.wait()
    inverse_lower_in.wait()
    lead_in = load(front.at[0, :, :, pl.ds(0, pivots)], lead, load_sem.at[2])
    inverse_upper_in = load(inverse_upper.at[0], inverse_upper_held, load_sem.at[3])
    trailing_of(0).start()
    trailing_of(1).start()

    def place(offset, part):
        start = at_row(*offset) * width + part * quarter
        return gathered.at[pl.ds(pl.multiple_of(start, 16), quarter)]

    numbers = {}
    sent = []

    def message(key, offset):
        _, part, axis, step = key
        number = numbers.setdefault(key, len(numbers))
        toward = (step, 0) if axis == 0 else (0, step)
        return pltpu.make_async_remote_copy(
            src_ref=place(offset, part),
            dst_ref=place(offset, part),
            send_sem=send_sem.at[number],
            recv_sem=recv_sem.at[number],
            device_id=(at_row(*toward), col_index),
            device_id_type=pl.DeviceIdType.MESH,
        )

    def send(offset, part, axis, step):
        seen = list(offset)
        seen[axis] -= step
        if seen[axis] == -2:
            seen[axis] = 2
        copy = message((tuple(seen), part, axis, step), offset)
        copy.start()
        sent.append(copy)

    def receive(offset, part, axis, step):
        message((offset, part, axis, step), offset).wait_recv()

    parts = ((0, 1), (2, 3))
    first = (1, 0)
    second = (0, 1)

    def offset_of(half, near, far):
        return (far, near) if half == 0 else (near, far)

    for part in (0, 2, 1, 3):
        span = pl.ds(part * quarter, quarter)
        permuted = jnp.dot(rows_held[span], chosen[...], preferred_element_type=jnp.float32)
        upper = lax.dot_general(
            permuted.astype(jnp.bfloat16),
            inverse_lower_held[...],
            NT,
            preferred_element_type=jnp.float32,
        )
        start = pl.multiple_of(row_index * width + part * quarter, 16)
        gathered[pl.ds(start, quarter)] = upper.astype(jnp.bfloat16)
        if part == 0:
            pl.semaphore_wait(barrier, len(near + across))
        half = part // 2
        for step in (1, -1):
            send((0, 0), part, first[half], step)
        for step in (1, -1):
            send((0, 0), part, second[half], step)
    own = pl.ds(pl.multiple_of(row_index * width, 16), width)
    upper_done = load(gathered.at[own], upper_out, store_sem.at[0])

    lead_in.wait()
    inverse_upper_in.wait()
    for s in range(slots):
        live = slot_block[col_index, row_index * slots + s] >= 0
        value = jnp.dot(lead[s], inverse_upper_held[...], preferred_element_type=jnp.float32)
        lower[pl.ds(s * block_rows, block_rows)] = jnp.where(live, value, 0.0).astype(jnp.bfloat16)
    lower_done = load(lower, lower_out, store_sem.at[1])

    live = [slot_block[col_index, row_index * slots + s] >= 0 for s in range(slots)]

    def turn(pair):
        trailing_of(pair).wait()

        def one(b, carry):
            columns = pl.ds(pl.multiple_of(b * block_rows, block_rows), block_rows)
            held = pl.ds((pair * pair_blocks + b) * 2, 2)
            for s in range(slots):
                turned = trailing[pair % 2, s, :, columns].T
                turned = jnp.where(live[s], turned, jnp.zeros_like(turned))
                child[held, :, pl.ds(s * block_rows, block_rows)] = turned.reshape(
                    2, piece, block_rows
                )
            return carry

        lax.fori_loop(0, pair_blocks, one, 0)
        if pair + 2 < pairs:
            trailing_of(pair + 2).start()

    def update(dz, dx):
        chunk = at_row(dz, dx)
        span = pl.ds(pl.multiple_of(chunk * width, 16), width)
        held = pl.ds(chunk * (width // piece), width // piece)
        product = lax.dot_general(
            gathered[span], lower[...], NT, preferred_element_type=jnp.float32
        ).reshape(width // piece, piece, lanes)
        child[held] = (child[held].astype(jnp.float32) - product).astype(jnp.bfloat16)

    def each():
        for k in range(2):
            for half in range(2):
                for step in (1, -1):
                    yield k, half, step, parts[half][k]

    def relay(near):
        for k, half, step, part in each():
            offset = offset_of(half, near, -step)
            receive(offset, part, second[half], step)
            if (k == 0) == (step == 1):
                send(offset, part, second[half], step)

    def finish(near):
        for k in range(2):
            for half in range(2):
                step = 1 if k == 0 else -1
                receive(offset_of(half, near, 2), parts[half][k], second[half], step)

    turn(0)
    for k, half, step, part in each():
        offset = offset_of(half, -step, 0)
        receive(offset, part, first[half], step)
        if (k == 0) == (step == 1):
            send(offset, part, first[half], step)
        for other in (1, -1):
            send(offset, part, second[half], other)
    turn(1)
    relay(0)
    turn(2)
    for k in range(2):
        for half in range(2):
            step = 1 if k == 0 else -1
            offset = offset_of(half, 2, 0)
            receive(offset, parts[half][k], first[half], step)
            for other in (1, -1):
                send(offset, parts[half][k], second[half], other)
    turn(3)
    turn(4)
    turn(5)
    relay(-1)
    turn(6)
    turn(7)
    fronts, columns = slot_rows.shape[0], table.shape[1]
    for f in range(fronts):
        table[f : f + 1] = place_row(slot_rows[f : f + 1], parent_map[f : f + 1], columns)
    own_map = parent_map[pl.ds(col_index, 1)]
    table[fronts : fronts + 1] = source_row(own_map, columns)
    table_done = load(table, table_out, store_sem.at[3])
    source_done = load(table, source, store_sem.at[4])
    relay(1)
    update(0, 0)
    for step in (1, -1):
        update(0, step)
        update(step, 0)
    finish(0)
    relay(2)
    for dz in (1, -1):
        for dx in (1, -1):
            update(dz, dx)
    update(0, 2)
    update(2, 0)
    finish(-1)
    finish(1)
    for step in (1, -1):
        update(step, 2)
        update(2, step)
    finish(2)
    update(2, 2)

    me = row_index * 8 + col_index
    source_done.wait()

    def fill(other):
        at = source[fronts, other // 2]
        value = child[jnp.maximum(at, 0) * 2 + lax.rem(other, 2)]
        spread[other] = jnp.where(at >= 0, value, jnp.zeros_like(value))

    def push(number, carry):
        other = partner(lax.rem(number * 101, devices))
        to = other[0] * 8 + other[1]
        fill(to)
        pltpu.make_async_remote_copy(
            src_ref=spread.at[to],
            dst_ref=arrived.at[me],
            send_sem=push_sem,
            recv_sem=land_sem,
            device_id=other,
            device_id_type=pl.DeviceIdType.MESH,
        ).start()
        return carry

    lax.fori_loop(1, devices, push, 0)
    fill(me)
    kept = load(spread.at[me], arrived.at[me], store_sem.at[2])
    for copy in sent:
        copy.wait_send()
    upper_done.wait()
    lower_done.wait()
    table_done.wait()
    kept.wait()
    others = pl.ds(0, devices - 1)
    pushed = pltpu.make_async_remote_copy(
        src_ref=spread.at[others],
        dst_ref=arrived.at[others],
        send_sem=push_sem,
        recv_sem=land_sem,
        device_id=partner(1),
        device_id_type=pl.DeviceIdType.MESH,
    )
    pushed.wait_send()
    pushed.wait_recv()


def factor_update(slot_block, parent_map, order, rows, inverse_lower, inverse_upper, front, devices):
    pivots = inverse_lower.shape[1]
    width = rows.shape[1]
    slots, block_rows, size = front.shape[1:]
    lanes = slots * block_rows
    piece = 64
    table = (16, 128)
    smem = pl.BlockSpec(memory_space=pltpu.SMEM)
    anywhere = pl.BlockSpec(memory_space=pl.ANY)
    operands = (slot_block, parent_map, order, rows, inverse_lower, inverse_upper, front)
    return pl.pallas_call(
        factor_update_exchange,
        out_shape=(
            jax.ShapeDtypeStruct((width, pivots), jnp.bfloat16),
            jax.ShapeDtypeStruct((lanes, pivots), jnp.bfloat16),
            pltpu.VMEM((devices, piece, lanes), jnp.bfloat16),
            jax.ShapeDtypeStruct(table, jnp.int32),
        ),
        in_specs=[
            smem,
            anywhere,
            anywhere,
            anywhere,
            anywhere,
            anywhere,
            anywhere,
            anywhere,
        ],
        out_specs=(
            anywhere,
            anywhere,
            pl.BlockSpec(memory_space=pltpu.VMEM),
            anywhere,
        ),
        scratch_shapes=[
            pltpu.VMEM((size - pivots, pivots), jnp.bfloat16),
            pltpu.VMEM(((size - pivots) // piece, piece, lanes), jnp.bfloat16),
            pltpu.VMEM((devices, piece, lanes), jnp.bfloat16),
            pltpu.VMEM((pivots, pivots), jnp.bfloat16),
            pltpu.VMEM((width, pivots), jnp.bfloat16),
            pltpu.VMEM((pivots, pivots), jnp.bfloat16),
            pltpu.VMEM((pivots, pivots), jnp.bfloat16),
            pltpu.VMEM((slots, block_rows, pivots), jnp.bfloat16),
            pltpu.VMEM((lanes, pivots), jnp.bfloat16),
            pltpu.VMEM((2, slots, block_rows, 2 * width), jnp.bfloat16),
            pltpu.VMEM(table, jnp.int32),
            pltpu.VMEM(slot_block.shape, jnp.int32),
            pltpu.VMEM(parent_map.shape, jnp.int32),
            pltpu.VMEM(order.shape, jnp.int32),
            pltpu.SMEM(table, jnp.int32),
            pltpu.SemaphoreType.DMA((60,)),
            pltpu.SemaphoreType.DMA((60,)),
            pltpu.SemaphoreType.DMA((7,)),
            pltpu.SemaphoreType.DMA((2,)),
            pltpu.SemaphoreType.DMA((5,)),
            pltpu.SemaphoreType.DMA,
            pltpu.SemaphoreType.DMA,
        ],
        compiler_params=pltpu.CompilerParams(
            collective_id=0, has_side_effects=True, vmem_limit_bytes=43 * MIB
        ),
    )(slot_block, *map(in_hbm, operands))


def assemble_kernel(
    place,
    arrived,
    initial,
    upper,
    lower,
    out,
    upper_out,
    lower_out,
    total,
    store_sem,
):
    parents, _, order = initial.shape
    block_rows = 128
    slots = arrived.shape[3] // block_rows
    stores = [
        pltpu.make_async_copy(upper, upper_out, store_sem.at[parents * 2]),
        pltpu.make_async_copy(lower, lower_out, store_sem.at[parents * 2 + 1]),
    ]
    for copy in stores:
        copy.start()
    together = 4
    for parent in range(parents):

        def some(step, carry):
            blocks = [step * together + k for k in range(together)]
            at = [pl.ds(pl.multiple_of(b * block_rows, block_rows), block_rows) for b in blocks]
            terms = []
            for b, lanes in zip(blocks, at):
                term = [initial[parent, :, lanes]]
                for child in range(2):
                    source = place[parent * 2 + child, b]
                    row = lax.shift_right_logical(source, 2)
                    slot = lax.bitwise_and(source, slots - 1)
                    slot_lanes = pl.ds(pl.multiple_of(slot * block_rows, block_rows), block_rows)
                    term.append(arrived[row, 2 * parent + child, :, slot_lanes])
                terms.append(term)
            for lanes, (first, left, right) in zip(at, terms):
                both = left.astype(jnp.float32) + right.astype(jnp.float32)
                total[parent, :, lanes] = (first.astype(jnp.float32) + both).astype(jnp.bfloat16)
            return carry

        steps = order // block_rows // together // 2
        for half in range(2):
            lax.fori_loop(half * steps, (half + 1) * steps, some, 0, unroll=2)
            span = pl.ds(half * (order // 2), order // 2)
            store = pltpu.make_async_copy(
                total.at[parent, :, span],
                out.at[parent, :, span],
                store_sem.at[parent * 2 + half],
            )
            store.start()
            stores.append(store)
    for copy in stores:
        copy.wait()


def assemble(place, arrived, initial, upper, lower):
    parents = initial.shape[0]
    anywhere = pl.BlockSpec(memory_space=pl.ANY)
    vmem = pl.BlockSpec(memory_space=pltpu.VMEM)
    return pl.pallas_call(
        assemble_kernel,
        out_shape=(
            jax.ShapeDtypeStruct(initial.shape, initial.dtype),
            jax.ShapeDtypeStruct(upper.shape, upper.dtype),
            jax.ShapeDtypeStruct(lower.shape, lower.dtype),
        ),
        in_specs=[pl.BlockSpec(memory_space=pltpu.SMEM), vmem, vmem, vmem, vmem],
        out_specs=(anywhere, anywhere, anywhere),
        scratch_shapes=[
            pltpu.VMEM(initial.shape, initial.dtype),
            pltpu.SemaphoreType.DMA((parents * 2 + 2,)),
        ],
        compiler_params=pltpu.CompilerParams(vmem_limit_bytes=8 * MIB),
    )(place, arrived, initial, upper, lower)


def shards(
    pivot_rows,
    pivot_order,
    inverse_lower,
    inverse_upper,
    front_rows,
    slot_block,
    parent_map,
    parent_init,
):
    rows, cols = lax.axis_size("row"), lax.axis_size("col")
    upper, lower, arrived, place = factor_update(
        slot_block,
        parent_map,
        pivot_order,
        jnp.swapaxes(pivot_rows, 1, 2),
        inverse_lower,
        inverse_upper,
        front_rows,
        rows * cols,
    )
    assembled, upper, lower = assemble(
        place, arrived.reshape(rows, cols, *arrived.shape[1:]), parent_init, upper, lower
    )
    return (lower.reshape(*front_rows.shape[:3], -1), upper.T[None], assembled)


def solution(mesh):
    return jax.shard_map(
        shards,
        mesh=mesh,
        in_specs=(
            P("col", None, "row"),
            P("col", None),
            P("col", None, None),
            P("col", None, None),
            P("col", "row", None, None),
            P(),
            P(),
            P(None, ("row", "col"), None),
        ),
        out_specs=(
            P("col", "row", None, None),
            P("col", None, "row"),
            P(None, ("row", "col"), None),
        ),
        check_vma=False,
    )
```
